256 devices in a mesh: pair: 64 (over x, z_hi, y, core), virt: 4 (over z_lo).
Axes of the slice: x: 4, y: 4, z: 8 (z_hi: 2, z_lo: 4; z = z_hi * 4 + z_lo), core: 2. Of those that a mesh axis runs over, the one named last changes fastest.
Arguments:
- amplitudes: bfloat16 [128, 128, 8, 4096], P('pair', None, 'virt'), may hold values from -6 to 6
- integrals: bfloat16 [8, 4096, 512], P('virt', 'pair'), may hold values from -0.0546875 to 0.0546875
- screen: int32 [128, 8], P('pair', 'virt'), may hold values 0 or 1
- irreps: int32 [16], replicated, may hold values from 0 to 1
- slab_index: int32 [9, 2], replicated, may hold values from 0 to 15, as said below
Outputs:
- ladder: bfloat16 [128, 128, 512], P('pair', None, 'virt')
The draws below stay inside these ranges and needn't reach their ends.
Inputs may be any that keep to these rules, and one draw needn't show every extreme that they name: `slab_index`: rows 2m + 1 and 2m + 2 name the same two tiles in opposite order, so that contraction tile pair k XOR 1 is the mirror of k.
All inputs are finite; a program needn't handle non-finite values. No bound on the sum of `screen` on one device may be relied on, other than what follows from the above.
Results may differ from the reference program's by a relative error of at most 0.00105.
Values may be sent and summed in bfloat16 or wider, within the bound.
A program may use at most 128 MiB of HBM per device.

```python
import jax
import jax.numpy as jnp

TILE = 64
NTILE = 16
NIRR = 2
NOCC = 128
KP = 8
ABCOL = 512


def draw_slab_index(key, part):
    key = jax.random.fold_in(key, 11)
    key_tiles, key_place = jax.random.split(key)
    halves = KP // 2
    tiles = jax.random.randint(key_tiles, (halves + 1, 2), 0, NTILE)
    place = jax.random.randint(key_place, (), 1, halves + 1)
    row_ids = jnp.arange(halves + 1)[:, None]
    ends = jnp.array([[0, NTILE - 1]], jnp.int32)
    tiles = jnp.where(row_ids == place, ends, tiles)
    head = tiles[:1]
    body_pairs = tiles[1:]
    pairs = jnp.stack([body_pairs, body_pairs[:, ::-1]], axis=1).reshape(KP, 2)
    return jnp.concatenate([head, pairs], axis=0).astype(jnp.int32)


def plant(drawn, key, smallest, high):
    index_at = [jax.random.randint(jax.random.fold_in(key, axis), (), 0, length) for axis, length in enumerate(drawn.shape)]
    longest = drawn.shape.index(max(drawn.shape))
    neighbour = index_at[:longest] + [(index_at[longest] + 1) % drawn.shape[longest]] + index_at[longest + 1:]
    return drawn.at[tuple(index_at)].set(smallest).at[tuple(neighbour)].set(high)


def levels(own_key, extent, cuts, smallest, high):
    level, own = 1.0, jax.random.fold_in(own_key, 6)
    for position, shards_of in cuts:
        heights = jnp.exp(jax.random.uniform(jax.random.fold_in(own, position), (shards_of,), jnp.float32, smallest / len(cuts), high / len(cuts)))
        level = level * jnp.repeat(heights, extent[position] // shards_of).reshape([-1 if axis == position else 1 for axis in range(len(extent))])
    return level


def centred(stream_key, shape, width, limit, shards=(), dtype=jnp.bfloat16):
    drawn = width * jax.random.normal(stream_key, shape, jnp.float32)
    if shards:
        drawn = drawn * levels(stream_key, shape, shards, -0.22, 0.18)
    return jnp.clip(drawn, -limit, limit).astype(dtype)


def setup_inputs(seed: int = 0) -> dict:
    key_of = jax.random.split(jax.random.key(seed), 6)
    return {
        "amplitudes": centred(key_of[0], (NOCC, NOCC, KP, TILE * TILE), 1.0, 6.0, ((0, 64), (2, 4))),
        "integrals": centred(key_of[1], (KP, TILE * TILE, ABCOL), (3 * KP * TILE * TILE // 8) ** -0.5, 0.0546875, ((0, 4), (1, 64))),
        "screen": plant((jax.random.randint(key_of[2], (NOCC, KP), 0, 4) < 3).astype(jnp.int32), jax.random.fold_in(key_of[2], 1), 0, 1),
        "irreps": plant(jax.random.randint(key_of[3], (NTILE,), 0, NIRR), jax.random.fold_in(key_of[3], 1), 0, NIRR - 1).astype(jnp.int32),
        "slab_index": draw_slab_index(jax.random.fold_in(key_of[5], 71), 0),
    }


def reference(amplitudes, integrals, screen, irreps, slab_index):
    occupied = amplitudes.shape[0]
    labels = irreps[slab_index]
    parity = (labels[1:, 0] + labels[1:, 1] + labels[0, 0] + labels[0, 1]) % 2
    allowed = (parity == 0).astype(jnp.float32)
    gates = screen.astype(jnp.float32)
    direct = jnp.zeros((occupied, occupied, ABCOL), jnp.float32)
    mirror = jnp.zeros((occupied, occupied, ABCOL), jnp.float32)
    for slab_panel in range(KP):
        mirror_panel = slab_panel ^ 1
        panel_weight = integrals[slab_panel]
        plain_rows = amplitudes[:, :, slab_panel, :].reshape(occupied * occupied, TILE * TILE)
        flipped = amplitudes[:, :, mirror_panel, :].reshape(occupied, occupied, TILE, TILE)
        flipped = flipped.transpose(0, 1, 3, 2).reshape(occupied * occupied, TILE * TILE)
        gate_plain = allowed[slab_panel] * gates[:, slab_panel]
        gate_flip = allowed[slab_panel] * gates[:, mirror_panel]
        plain_term = jnp.dot(plain_rows, panel_weight, preferred_element_type=jnp.float32)
        flip_term = jnp.dot(flipped, panel_weight, preferred_element_type=jnp.float32)
        direct = direct + gate_plain[:, None, None] * plain_term.reshape(occupied, occupied, ABCOL)
        mirror = mirror + gate_flip[:, None, None] * flip_term.reshape(occupied, occupied, ABCOL)
    return (0.5 * (direct + mirror.transpose(1, 0, 2))).astype(jnp.bfloat16)
```

```python
import jax
import jax.numpy as jnp
from jax import lax
from jax.experimental import pallas as pl
from jax.experimental.pallas import tpu as pltpu
from jax.sharding import PartitionSpec as P

TILE = 64
STAGES = 4
LANES = 128
MESH = pl.DeviceIdType.MESH

RING1, RING1_FAR, RING2, RING2_FAR, CROSS = 0, 2, 4, 12, 14
COPIES = 18


def pair_index(x, h, y, core):
    return ((x * 2 + h) * 4 + y) * 2 + core


def kernel(
    slab_ref, irreps_ref, screen_ref, own_ref, other_ref, amp_ref, out_ref,
    panels, plain, flipped, turned, partial, arrived, mirror_sum, tiles_out, tiles_in, result,
    local_sem, amp_sem, send_sem, recv_sem, sum_send, sum_recv, tile_send, tile_recv,
):
    pair = lax.axis_index("pair")
    virt = lax.axis_index("virt")
    core = lax.rem(pair, 2)
    y = lax.rem(pair // 2, 4)
    h = lax.rem(pair // 8, 2)
    x = pair // 16
    first = x * (1 - core) + y * core
    second = y * (1 - core) + x * core

    def at(first_pos, second_pos, which_core):
        px = first_pos * (1 - core) + second_pos * core
        py = second_pos * (1 - core) + first_pos * core
        return (pair_index(px, h, py, which_core), virt)

    def around(position, step):
        return lax.rem(position + step, 4)

    first_up, first_down = around(first, 1), around(first, 3)
    second_up, second_down = around(second, 1), around(second, 3)
    first_far, second_far = around(first, 2), around(second, 2)
    blocks = (3 * (1 - virt // 2), lax.rem(2 + 3 * virt, 5), 1 + lax.rem(virt, 2), virt)

    loads = {}
    for panel in range(2):
        for i in range(2):
            loads[panel, i] = pltpu.make_async_copy(
                amp_ref.at[panel, i], plain.at[panel, i], amp_sem.at[panel * 2 + i]
            )
    local = {}
    for q in range(STAGES):
        columns = pl.ds(pl.multiple_of(blocks[q] * LANES, LANES), LANES)
        for n, (ref, level) in enumerate(((own_ref, h), (other_ref, 1 - h))):
            local[q, n] = pltpu.make_async_copy(
                ref.at[:, :, columns],
                panels.at[q, core, second, first, level],
                local_sem.at[q * 2 + n],
            )
            local[q, n].start()
    for load in loads.values():
        load.start()

    barrier = pltpu.get_barrier_semaphore()

    def greet(step, carry):
        pl.semaphore_signal(
            barrier, inc=1, device_id=(lax.rem(pair + step, 64), virt), device_id_type=MESH
        )
        return carry

    lax.fori_loop(1, 64, greet, 0)
    for step in range(1, 4):
        pl.semaphore_signal(
            barrier, inc=1, device_id=(pair, lax.rem(virt + step, 4)), device_id_type=MESH
        )
    pl.semaphore_wait(barrier, 66)

    sent = []

    def block(q, first_pos, second_pos):
        return panels.at[q, core, second_pos, first_pos]

    def half(q, first_pos, second_pos, level):
        return panels.at[q, core, second_pos, first_pos, level]

    def column(q, second_pos):
        return panels.at[q, core, second_pos]

    def column_half(q, second_pos, level):
        return panels.at[q, core, second_pos, :, level]

    def copy(q, number, ref, device):
        return pltpu.make_async_remote_copy(
            src_ref=ref,
            dst_ref=ref,
            send_sem=send_sem.at[q, number],
            recv_sem=recv_sem.at[q, number],
            device_id=device,
            device_id_type=MESH,
        )

    def send(q, number, ref, device):
        moved = copy(q, number, ref, device)
        moved.start()
        sent.append(moved)

    def receive(q, number, ref):
        copy(q, number, ref, at(first, second, 1 - core)).wait_recv()

    def both_ways(q, slot, first_pos):
        send(q, RING2 + slot * 2, block(q, first_pos, second), at(first, second_up, core))
        send(q, RING2 + slot * 2 + 1, block(q, first_pos, second), at(first, second_down, core))

    def cross(q, number, second_pos):
        send(q, CROSS + number, column(q, second_pos), at(first, second, 1 - core))

    def begin(q):
        local[q, 0].wait()
        local[q, 1].wait()
        send(q, RING1, block(q, first, second), at(first_up, second, core))
        send(q, RING1 + 1, block(q, first, second), at(first_down, second, core))
        both_ways(q, 0, first)

    def near(q):
        receive(q, RING1, block(q, first_down, second))
        send(q, RING1_FAR, half(q, first_down, second, 0), at(first_up, second, core))
        both_ways(q, 1, first_down)
        receive(q, RING1 + 1, block(q, first_up, second))
        send(q, RING1_FAR + 1, half(q, first_up, second, 1), at(first_down, second, core))
        both_ways(q, 2, first_up)

    def far(q):
        receive(q, RING1_FAR, half(q, first_far, second, 0))
        receive(q, RING1_FAR + 1, half(q, first_far, second, 1))
        both_ways(q, 3, first_far)
        cross(q, 0, second)

    def near_columns(q):
        order = (first, first_down, first_up, first_far)
        for way, (source, level, target) in enumerate(
            ((second_down, 0, second_up), (second_up, 1, second_down))
        ):
            for slot in range(4):
                receive(q, RING2 + slot * 2 + way, block(q, order[slot], source))
            send(q, RING2_FAR + way, column_half(q, source, level), at(first, target, core))
            cross(q, 1 + way, source)

    def far_columns(q):
        receive(q, RING2_FAR, column_half(q, second_far, 0))
        receive(q, RING2_FAR + 1, column_half(q, second_far, 1))
        cross(q, 3, second_far)

    def complete(q):
        mine = (second, second_down, second_up, second_far)
        for number in range(4):
            copy(q, CROSS + number, column(q, mine[number]), at(first, second, 1 - core)).wait_recv()

    def label(row, side):
        return irreps_ref[slab_ref[row, side]]

    target_label = label(0, 0) + label(0, 1)

    def gate(panel, i):
        row = virt * 2 + panel + 1
        parity = lax.rem(label(row, 0) + label(row, 1) + target_label, 2)
        return (screen_ref[i, panel] * (1 - parity)).astype(jnp.float32)

    def gate_part(panel, i, start, stop):
        level = gate(panel, i)

        def step(m, carry):
            lanes = pl.ds(pl.multiple_of(m * LANES, LANES), LANES)
            block_rows = plain[panel, i, :, lanes].astype(jnp.float32) * level
            plain[panel, i, :, lanes] = block_rows.astype(jnp.bfloat16)
            turned[lanes, :] = block_rows.T
            return carry

        lax.fori_loop(start, stop, step, 0)

    def flip_part(panel, i, start, stop):
        def step(m, carry):
            even = turned[pl.ds(2 * m, TILE, stride=TILE), :]
            odd = turned[pl.ds(2 * m + 1, TILE, stride=TILE), :]
            lanes = pl.ds(pl.multiple_of(m * LANES, LANES), LANES)
            both = jnp.concatenate([even, odd], axis=0).T
            flipped[1 - panel, i, :, lanes] = both.astype(jnp.bfloat16)
            return carry

        lax.fori_loop(start, stop, step, 0)

    parts = []
    for panel in range(2):
        for i in range(2):
            for start in (0, 16):
                parts.append((gate_part, panel, i, start))
            for start in (0, 16):
                parts.append((flip_part, panel, i, start))
    loaded = set()

    def prepare(count):
        for _ in range(count):
            if not parts:
                return
            part, panel, i, start = parts.pop(0)
            if (panel, i) not in loaded:
                loaded.add((panel, i))
                loads[panel, i].wait()
            part(panel, i, start, start + 16)

    def multiply(q, rows_of):
        for rows in rows_of:
            partial[q, rows] = jnp.zeros((256, LANES), jnp.float32)

        def step(n, carry):
            panel, at_x = n // 4, lax.rem(n, 4)
            cells = []
            for level in range(2):
                for at_y in range(4):
                    cells.append(panels[q, 0, at_y, at_x, level, panel])
                    cells.append(panels[q, 1, at_x, at_y, level, panel])
            right = jnp.concatenate(cells, axis=0)
            lanes = pl.ds(pl.multiple_of(at_x * 1024, 1024), 1024)
            for rows in rows_of:
                source = (plain, flipped)[rows]
                left = source[panel, :, :, lanes].reshape(256, 1024)
                partial[q, rows] += jnp.dot(left, right, preferred_element_type=jnp.float32)
            return carry

        lax.fori_loop(0, 8, step, 0)

    sums = []

    def pass_on(q):
        moved = pltpu.make_async_remote_copy(
            src_ref=partial.at[q],
            dst_ref=arrived.at[virt],
            send_sem=sum_send.at[q],
            recv_sem=sum_recv.at[virt],
            device_id=(pair, blocks[q]),
            device_id_type=MESH,
        )
        moved.start()
        sums.append(moved)

    begin(0)
    begin(1)
    prepare(2)
    near(0)
    prepare(2)
    far(0)
    begin(2)
    near(1)
    prepare(2)
    near_columns(0)
    far(1)
    prepare(2)
    far_columns(0)
    begin(3)
    near(2)
    prepare(2)
    near_columns(1)
    far(2)
    prepare(2)
    far_columns(1)
    near(3)
    prepare(len(parts))
    complete(0)
    multiply(0, (1, 0))
    pass_on(0)
    near_columns(2)
    far(3)
    complete(1)
    multiply(1, (1, 0))
    pass_on(1)
    far_columns(2)
    near_columns(3)
    complete(2)
    multiply(2, (1, 0))
    pass_on(2)
    far_columns(3)
    complete(3)
    multiply(3, (1,))

    others = [lax.rem(virt + step, 4) for step in range(1, 4)]
    for other in others:
        pltpu.make_async_remote_copy(
            src_ref=partial.at[0],
            dst_ref=arrived.at[other],
            send_sem=sum_send.at[0],
            recv_sem=sum_recv.at[other],
            device_id=(pair, other),
            device_id_type=MESH,
        ).wait_recv()
    mirror_sum[...] = partial[3, 1] + (
        arrived[others[0], 1] + arrived[others[1], 1] + arrived[others[2], 1]
    )
    for which in range(2):
        for i in range(2):
            for j in range(2):
                rows = mirror_sum[pl.ds(i * 128 + which * 2 + j, 32, stride=4), :]
                tiles_out[pl.ds(which * 4 + i * 2 + j, 32, stride=8), :] = rows

    def tile_copy(target):
        return pltpu.make_async_remote_copy(
            src_ref=tiles_out.at[pl.ds(pl.multiple_of((target // 2) * 8, 8), 8)],
            dst_ref=tiles_in.at[pl.ds(pl.multiple_of(pair * 8, 8), 8)],
            send_sem=tile_send,
            recv_sem=tile_recv,
            device_id=(target, virt),
            device_id_type=MESH,
        )

    def exchange(step, carry):
        tile_copy(lax.rem(pair + step, 64)).start()
        return carry

    lax.fori_loop(1, 64, exchange, 0)
    tiles_in[pl.ds(pl.multiple_of(pair * 8, 8), 8), :] = tiles_out[
        pl.ds(pl.multiple_of((pair // 2) * 8, 8), 8), :
    ]
    multiply(3, (0,))
    partial[3, 0] += arrived[others[0], 0] + arrived[others[1], 0] + arrived[others[2], 0]

    everything = pltpu.make_async_remote_copy(
        src_ref=tiles_in.at[pl.ds(0, 63 * 8)],
        dst_ref=tiles_in.at[pl.ds(0, 63 * 8)],
        send_sem=tile_send,
        recv_sem=tile_recv,
        device_id=(lax.rem(pair + 1, 64), virt),
        device_id_type=MESH,
    )
    everything.wait_recv()
    for i in range(2):
        for j in range(2):
            direct = partial[3, 0, pl.ds(i * 128 + j, 64, stride=2), :]
            mirrored = tiles_in[pl.ds(core * 4 + j * 2 + i, 64, stride=8), :]
            result[pl.ds(i * 128 + j, 64, stride=2), :] = 0.5 * (direct + mirrored)
    out_ref[...] = result[...].astype(jnp.bfloat16).reshape(2, 128, LANES)

    everything.wait_send()
    for moved in sums:
        moved.wait_send()
    for moved in sent:
        moved.wait_send()


def body(amplitudes, integrals, screen, irreps, slab_index):
    swap = [(p, p ^ 8) for p in range(64)]
    other = lax.ppermute(integrals, "pair", swap)
    rows = amplitudes.transpose(2, 0, 1, 3)
    smem = pl.BlockSpec(memory_space=pltpu.SMEM)
    anywhere = pl.BlockSpec(memory_space=pl.ANY)
    vmem = pl.BlockSpec(memory_space=pltpu.VMEM)
    dma, f32, bf16 = pltpu.SemaphoreType.DMA, jnp.float32, jnp.bfloat16
    return pl.pallas_call(
        kernel,
        out_shape=jax.ShapeDtypeStruct((2, 128, LANES), bf16),
        in_specs=[smem, smem, smem, anywhere, anywhere, anywhere],
        out_specs=vmem,
        scratch_shapes=[
            pltpu.VMEM((STAGES, 2, 4, 4, 2, 2, TILE, LANES), bf16),
            pltpu.VMEM((2, 2, 128, 4096), bf16),
            pltpu.VMEM((2, 2, 128, 4096), bf16),
            pltpu.VMEM((4096, 128), f32),
            pltpu.VMEM((STAGES, 2, 256, LANES), f32),
            pltpu.VMEM((4, 2, 256, LANES), f32),
            pltpu.VMEM((256, LANES), f32),
            pltpu.VMEM((32 * 8, LANES), f32),
            pltpu.VMEM((64 * 8, LANES), f32),
            pltpu.VMEM((256, LANES), f32),
            dma((STAGES * 2,)),
            dma((4,)),
            dma((STAGES, COPIES)),
            dma((STAGES, COPIES)),
            dma((STAGES,)),
            dma((4,)),
            dma,
            dma,
        ],
        compiler_params=pltpu.CompilerParams(
            collective_id=0, has_side_effects=True, vmem_limit_bytes=40 * 1024 * 1024
        ),
        cost_estimate=pl.CostEstimate(
            flops=2 * 512 * 8192 * 512, bytes_accessed=5 << 20, transcendentals=0
        ),
    )(slab_index, irreps, screen, integrals, other, rows)


def solution(mesh):
    in_specs = (P("pair", None, "virt", None), P("virt", "pair", None), P("pair", "virt"), P(), P())
    out_specs = P("pair", None, "virt")
    return jax.shard_map(body, mesh=mesh, in_specs=in_specs, out_specs=out_specs, check_vma=False)
```

```python
import jax
import jax.numpy as jnp
from jax import lax
from jax.experimental import pallas as pl
from jax.experimental.pallas import tpu as pltpu
from jax.sharding import PartitionSpec as P

TILE = 64
STAGES = 4
LANES = 128
MESH = pl.DeviceIdType.MESH

RING1, RING1_FAR, RING2, RING2_NEAR, RING2_FAR, ACROSS, CROSS, LEVEL = 0, 4, 6, 10, 12, 14, 16, 20
COPIES = 21
OWN, UP, DOWN, FAR = 0, 1, 2, 3


def pair_index(x, h, y, core):
    return ((x * 2 + h) * 4 + y) * 2 + core


def kernel(
    slab_ref, irreps_ref, screen_ref, own_ref, amp_ref, out_ref,
    panels, plain, flipped, turned, partial, arrived, mirror_sum, tiles_out, tiles_in, result,
    local_sem, amp_sem, send_sem, recv_sem, sum_send, sum_recv, tile_send, tile_recv,
):
    pair = lax.axis_index("pair")
    virt = lax.axis_index("virt")
    core = lax.rem(pair, 2)
    y = lax.rem(pair // 2, 4)
    h = lax.rem(pair // 8, 2)
    x = pair // 16
    first = x * (1 - core) + y * core
    second = y * (1 - core) + x * core

    def at(first_pos, second_pos, level, which_core):
        px = first_pos * (1 - core) + second_pos * core
        py = second_pos * (1 - core) + first_pos * core
        return (pair_index(px, level, py, which_core), virt)

    def around(position, step):
        return lax.rem(position + step, 4)

    first_up = at(around(first, 1), second, h, core)
    first_down = at(around(first, 3), second, h, core)
    second_up = at(first, around(second, 1), h, core)
    second_down = at(first, around(second, 3), h, core)
    sibling = at(first, second, h, 1 - core)
    opposite = at(first, second, 1 - h, core)
    blocks = (3 * (1 - virt // 2), lax.rem(2 + 3 * virt, 5), 1 + lax.rem(virt, 2), virt)

    loads = {}
    for panel in range(2):
        for i in range(2):
            loads[panel, i] = pltpu.make_async_copy(
                amp_ref.at[panel, i], plain.at[panel, i], amp_sem.at[panel * 2 + i]
            )
    local = {}
    for q in range(STAGES):
        columns = pl.ds(pl.multiple_of(blocks[q] * LANES, LANES), LANES)
        local[q] = pltpu.make_async_copy(
            own_ref.at[:, :, columns], panels.at[q, core, OWN, OWN, h], local_sem.at[q]
        )
        local[q].start()
    for load in loads.values():
        load.start()

    barrier = pltpu.get_barrier_semaphore()
    along = [(pair, lax.rem(virt + step, 4)) for step in range(1, 4)]
    for device in [first_up, first_down, second_up, second_down, sibling, opposite] + along:
        pl.semaphore_signal(barrier, inc=1, device_id=device, device_id_type=MESH)
    pl.semaphore_wait(barrier, 9)

    sent = []

    def copy(q, number, source, target, device):
        return pltpu.make_async_remote_copy(
            src_ref=panels.at[(q, core) + source],
            dst_ref=panels.at[(q, core) + target],
            send_sem=send_sem.at[q, number],
            recv_sem=recv_sem.at[q, number],
            device_id=device,
            device_id_type=MESH,
        )

    def send(q, number, source, target, device):
        moved = copy(q, number, source, target, device)
        moved.start()
        sent.append(moved)

    def receive(q, number, target):
        copy(q, number, target, target, sibling).wait_recv()

    def start_level(q, which, level):
        send(q, RING1 + which, (OWN, OWN, level), (OWN, DOWN, level), first_up)
        send(q, RING1 + which + 2, (OWN, OWN, level), (OWN, UP, level), first_down)
        send(q, RING2 + which, (OWN, OWN, level), (DOWN, OWN, level), second_up)
        send(q, RING2 + which + 2, (OWN, OWN, level), (UP, OWN, level), second_down)

    def begin(q):
        local[q].wait()
        send(q, LEVEL, (OWN, OWN, h), (OWN, OWN, h), opposite)
        start_level(q, 0, h)

    def begin_other(q):
        receive(q, LEVEL, (OWN, OWN, 1 - h))
        start_level(q, 1, 1 - h)

    near_two = pl.ds(UP, 2)

    def near(q):
        for which, level in enumerate((h, 1 - h)):
            receive(q, RING1 + which, (OWN, DOWN, level))
            receive(q, RING1 + which + 2, (OWN, UP, level))
        send(q, RING1_FAR, (OWN, DOWN, h), (OWN, FAR, h), first_up)
        send(q, RING1_FAR + 1, (OWN, UP, 1 - h), (OWN, FAR, 1 - h), first_down)
        send(q, RING2_NEAR, (OWN, near_two), (DOWN, near_two), second_up)
        send(q, RING2_NEAR + 1, (OWN, near_two), (UP, near_two), second_down)

    def far(q):
        receive(q, RING1_FAR, (OWN, FAR, h))
        receive(q, RING1_FAR + 1, (OWN, FAR, 1 - h))
        send(q, RING2_FAR, (OWN, FAR), (DOWN, FAR), second_up)
        send(q, RING2_FAR + 1, (OWN, FAR), (UP, FAR), second_down)
        send(q, CROSS, (OWN,), (OWN,), sibling)

    every = pl.ds(0, 4)

    def near_columns(q):
        for way, (side, level, target) in enumerate(
            ((DOWN, h, second_up), (UP, 1 - h, second_down))
        ):
            receive(q, RING2 + way * 2, (side, OWN, h))
            receive(q, RING2 + way * 2 + 1, (side, OWN, 1 - h))
            receive(q, RING2_NEAR + way, (side, near_two))
            receive(q, RING2_FAR + way, (side, FAR))
            send(q, ACROSS + way, (side, every, level), (FAR, every, level), target)
            send(q, CROSS + 1 + way, (side,), (side,), sibling)

    def far_columns(q):
        receive(q, ACROSS, (FAR, every, h))
        receive(q, ACROSS + 1, (FAR, every, 1 - h))
        send(q, CROSS + 3, (FAR,), (FAR,), sibling)

    def complete(q):
        for number in range(4):
            receive(q, CROSS + number, (number,))

    def label(row, side):
        return irreps_ref[slab_ref[row, side]]

    target_label = label(0, 0) + label(0, 1)

    def gate(panel, i):
        row = virt * 2 + panel + 1
        parity = lax.rem(label(row, 0) + label(row, 1) + target_label, 2)
        return (screen_ref[i, panel] * (1 - parity)).astype(jnp.float32)

    def unrolled(one, start, stop):
        def step(m, carry):
            for n in range(4):
                one(m * 4 + n)
            return carry

        lax.fori_loop(start // 4, stop // 4, step, 0)

    def gate_part(panel, i, start, stop):
        level = gate(panel, i)

        def one(m):
            lanes = pl.ds(pl.multiple_of(m * LANES, LANES), LANES)
            block_rows = plain[panel, i, :, lanes].astype(jnp.float32) * level
            plain[panel, i, :, lanes] = block_rows.astype(jnp.bfloat16)
            turned[lanes, :] = block_rows.T

        unrolled(one, start, stop)

    def flip_part(panel, i, start, stop):
        def one(m):
            even = turned[pl.ds(2 * m, TILE, stride=TILE), :]
            odd = turned[pl.ds(2 * m + 1, TILE, stride=TILE), :]
            lanes = pl.ds(pl.multiple_of(m * LANES, LANES), LANES)
            both = jnp.concatenate([even, odd], axis=0).T
            flipped[1 - panel, i, :, lanes] = both.astype(jnp.bfloat16)

        unrolled(one, start, stop)

    parts = []
    for panel in range(2):
        for i in range(2):
            for start in (0, 16):
                parts.append((gate_part, panel, i, start))
            for start in (0, 16):
                parts.append((flip_part, panel, i, start))
    loaded = set()

    def prepare(count):
        for _ in range(count):
            if not parts:
                return
            part, panel, i, start = parts.pop(0)
            if (panel, i) not in loaded:
                loaded.add((panel, i))
                loads[panel, i].wait()
            part(panel, i, start, start + 16)

    def place(position, centre):
        distance = lax.rem(position - centre + 4, 4)
        return distance + distance // 2 - 2 * (distance // 3)

    def multiply(q, rows_of):
        for rows in rows_of:
            partial[q, rows] = jnp.zeros((256, LANES), jnp.float32)

        def step(n, carry):
            panel, at_x = n // 4, lax.rem(n, 4)
            cells = []
            for level in range(2):
                for at_y in range(4):
                    near_x, near_y = place(at_x, x), place(at_y, y)
                    cells.append(panels[q, 0, near_y, near_x, level, panel])
                    cells.append(panels[q, 1, near_x, near_y, level, panel])
            right = jnp.concatenate(cells, axis=0)
            lanes = pl.ds(pl.multiple_of(at_x * 1024, 1024), 1024)
            for rows in rows_of:
                source = (plain, flipped)[rows]
                left = source[panel, :, :, lanes].reshape(256, 1024)
                partial[q, rows] += jnp.dot(left, right, preferred_element_type=jnp.float32)
            return carry

        lax.fori_loop(0, 8, step, 0)

    sums = []

    def pass_on(q):
        moved = pltpu.make_async_remote_copy(
            src_ref=partial.at[q],
            dst_ref=arrived.at[virt],
            send_sem=sum_send.at[q],
            recv_sem=sum_recv.at[virt],
            device_id=(pair, blocks[q]),
            device_id_type=MESH,
        )
        moved.start()
        sums.append(moved)

    for q in range(STAGES):
        begin(q)
    begin_other(0)
    prepare(2)
    begin_other(1)
    near(0)
    prepare(2)
    far(0)
    begin_other(2)
    near(1)
    prepare(2)
    begin_other(3)
    near_columns(0)
    far(1)
    prepare(2)
    far_columns(0)
    near(2)
    prepare(2)
    near_columns(1)
    far(2)
    prepare(2)
    far_columns(1)
    near(3)
    prepare(len(parts))
    complete(0)
    multiply(0, (1, 0))
    pass_on(0)
    near_columns(2)
    far(3)
    complete(1)
    multiply(1, (1, 0))
    pass_on(1)
    far_columns(2)
    near_columns(3)
    complete(2)
    multiply(2, (1, 0))
    pass_on(2)
    far_columns(3)
    complete(3)
    multiply(3, (1,))

    others = [lax.rem(virt + step, 4) for step in range(1, 4)]
    for other in others:
        pltpu.make_async_remote_copy(
            src_ref=partial.at[0],
            dst_ref=arrived.at[other],
            send_sem=sum_send.at[0],
            recv_sem=sum_recv.at[other],
            device_id=(pair, other),
            device_id_type=MESH,
        ).wait_recv()
    mirror_sum[...] = partial[3, 1] + (
        arrived[others[0], 1] + arrived[others[1], 1] + arrived[others[2], 1]
    )
    for which in range(2):
        for i in range(2):
            for j in range(2):
                rows = mirror_sum[pl.ds(i * 128 + which * 2 + j, 32, stride=4), :]
                tiles_out[pl.ds(which * 4 + i * 2 + j, 32, stride=8), :] = rows

    def tile_copy(target):
        return pltpu.make_async_remote_copy(
            src_ref=tiles_out.at[pl.ds(pl.multiple_of((target // 2) * 8, 8), 8)],
            dst_ref=tiles_in.at[pl.ds(pl.multiple_of(pair * 8, 8), 8)],
            send_sem=tile_send,
            recv_sem=tile_recv,
            device_id=(target, virt),
            device_id_type=MESH,
        )

    def exchange(step, carry):
        tile_copy(lax.rem(pair + step, 64)).start()
        return carry

    lax.fori_loop(1, 64, exchange, 0)
    tiles_in[pl.ds(pl.multiple_of(pair * 8, 8), 8), :] = tiles_out[
        pl.ds(pl.multiple_of((pair // 2) * 8, 8), 8), :
    ]
    multiply(3, (0,))
    partial[3, 0] += arrived[others[0], 0] + arrived[others[1], 0] + arrived[others[2], 0]

    everything = pltpu.make_async_remote_copy(
        src_ref=tiles_in.at[pl.ds(0, 63 * 8)],
        dst_ref=tiles_in.at[pl.ds(0, 63 * 8)],
        send_sem=tile_send,
        recv_sem=tile_recv,
        device_id=(lax.rem(pair + 1, 64), virt),
        device_id_type=MESH,
    )
    everything.wait_recv()
    for i in range(2):
        for j in range(2):
            direct = partial[3, 0, pl.ds(i * 128 + j, 64, stride=2), :]
            mirrored = tiles_in[pl.ds(core * 4 + j * 2 + i, 64, stride=8), :]
            result[pl.ds(i * 128 + j, 64, stride=2), :] = 0.5 * (direct + mirrored)
    out_ref[...] = result[...].astype(jnp.bfloat16).reshape(2, 128, LANES)

    everything.wait_send()
    for moved in sums:
        moved.wait_send()
    for moved in sent:
        moved.wait_send()


def body(amplitudes, integrals, screen, irreps, slab_index):
    rows = amplitudes.transpose(2, 0, 1, 3)
    smem = pl.BlockSpec(memory_space=pltpu.SMEM)
    anywhere = pl.BlockSpec(memory_space=pl.ANY)
    vmem = pl.BlockSpec(memory_space=pltpu.VMEM)
    dma, f32, bf16 = pltpu.SemaphoreType.DMA, jnp.float32, jnp.bfloat16
    return pl.pallas_call(
        kernel,
        out_shape=jax.ShapeDtypeStruct((2, 128, LANES), bf16),
        in_specs=[smem, smem, smem, anywhere, anywhere],
        out_specs=vmem,
        scratch_shapes=[
            pltpu.VMEM((STAGES, 2, 4, 4, 2, 2, TILE, LANES), bf16),
            pltpu.VMEM((2, 2, 128, 4096), bf16),
            pltpu.VMEM((2, 2, 128, 4096), bf16),
            pltpu.VMEM((4096, 128), f32),
            pltpu.VMEM((STAGES, 2, 256, LANES), f32),
            pltpu.VMEM((4, 2, 256, LANES), f32),
            pltpu.VMEM((256, LANES), f32),
            pltpu.VMEM((32 * 8, LANES), f32),
            pltpu.VMEM((64 * 8, LANES), f32),
            pltpu.VMEM((256, LANES), f32),
            dma((STAGES,)),
            dma((4,)),
            dma((STAGES, COPIES)),
            dma((STAGES, COPIES)),
            dma((STAGES,)),
            dma((4,)),
            dma,
            dma,
        ],
        compiler_params=pltpu.CompilerParams(
            collective_id=0, has_side_effects=True, vmem_limit_bytes=40 * 1024 * 1024
        ),
        cost_estimate=pl.CostEstimate(
            flops=2 * 512 * 8192 * 512, bytes_accessed=5 << 20, transcendentals=0
        ),
    )(slab_index, irreps, screen, integrals, rows)


def solution(mesh):
    in_specs = (P("pair", None, "virt", None), P("virt", "pair", None), P("pair", "virt"), P(), P())
    out_specs = P("pair", None, "virt")
    return jax.shard_map(body, mesh=mesh, in_specs=in_specs, out_specs=out_specs, check_vma=False)
```

```python
import jax
import jax.numpy as jnp
from jax import lax
from jax.experimental import pallas as pl
from jax.experimental.pallas import tpu as pltpu
from jax.sharding import PartitionSpec as P

TILE = 64
STAGES = 4
LANES = 128
MESH = pl.DeviceIdType.MESH

RING1, RING2, RING2_REST, ACROSS, CROSS, LEVEL = 0, 6, 10, 14, 16, 19
COPIES = 20
STEPS = 32000.0
OWN, UP, DOWN, FAR = 0, 1, 2, 3


def pair_index(x, h, y, core):
    return ((x * 2 + h) * 4 + y) * 2 + core


def kernel(
    slab_ref, irreps_ref, screen_ref, own_ref, amp_ref, out_ref,
    panels, amps, turned, partial, coded, scales, arrived, arrived_scales, mirror_sum, tiles_out, tiles_in, result,
    local_sem, amp_sem, send_sem, recv_sem, sum_send, sum_recv, tile_send, tile_recv,
):
    pair = lax.axis_index("pair")
    virt = lax.axis_index("virt")
    core = lax.rem(pair, 2)
    y = lax.rem(pair // 2, 4)
    h = lax.rem(pair // 8, 2)
    x = pair // 16
    first = x * (1 - core) + y * core
    second = y * (1 - core) + x * core

    def at(first_pos, second_pos, level, which_core):
        px = first_pos * (1 - core) + second_pos * core
        py = second_pos * (1 - core) + first_pos * core
        return (pair_index(px, level, py, which_core), virt)

    def around(position, step):
        return lax.rem(position + step, 4)

    first_up = at(around(first, 1), second, h, core)
    first_down = at(around(first, 3), second, h, core)
    first_far = at(around(first, 2), second, h, core)
    second_up = at(first, around(second, 1), h, core)
    second_down = at(first, around(second, 3), h, core)
    sibling = at(first, second, h, 1 - core)
    opposite = at(first, second, 1 - h, core)
    blocks = (3 * (1 - virt // 2), lax.rem(2 + 3 * virt, 5), 1 + lax.rem(virt, 2), virt)

    loads = {}
    for panel in range(2):
        for i in range(2):
            loads[panel, i] = pltpu.make_async_copy(
                amp_ref.at[panel, i], amps.at[panel, 0, i], amp_sem.at[panel * 2 + i]
            )
    local = {}
    for q in range(STAGES):
        columns = pl.ds(pl.multiple_of(blocks[q] * LANES, LANES), LANES)
        local[q] = pltpu.make_async_copy(
            own_ref.at[:, :, columns], panels.at[q, core, OWN, OWN, h], local_sem.at[q]
        )
        local[q].start()
    for load in loads.values():
        load.start()

    barrier = pltpu.get_barrier_semaphore()
    along = [(pair, lax.rem(virt + step, 4)) for step in range(1, 4)]
    for device in [first_up, first_down, first_far, second_up, second_down, sibling, opposite] + along:
        pl.semaphore_signal(barrier, inc=1, device_id=device, device_id_type=MESH)
    pl.semaphore_wait(barrier, 10)

    sent = []

    def copy(q, number, source, target, device):
        return pltpu.make_async_remote_copy(
            src_ref=panels.at[(q, core) + source],
            dst_ref=panels.at[(q, core) + target],
            send_sem=send_sem.at[q, number],
            recv_sem=recv_sem.at[q, number],
            device_id=device,
            device_id_type=MESH,
        )

    def send(q, number, source, target, device):
        moved = copy(q, number, source, target, device)
        moved.start()
        sent.append(moved)

    def receive(q, number, target):
        copy(q, number, target, target, sibling).wait_recv()

    def start_level(q, which, level):
        here = (OWN, OWN, level)
        send(q, RING1 + which * 3, here, (OWN, DOWN, level), first_up)
        send(q, RING1 + which * 3 + 1, here, (OWN, UP, level), first_down)
        send(q, RING1 + which * 3 + 2, here, (OWN, FAR, level), first_far)
        send(q, RING2 + which * 2, here, (DOWN, OWN, level), second_up)
        send(q, RING2 + which * 2 + 1, here, (UP, OWN, level), second_down)

    def begin(q):
        local[q].wait()
        send(q, LEVEL, (OWN, OWN, h), (OWN, OWN, h), opposite)
        start_level(q, 0, h)

    def begin_other(q):
        receive(q, LEVEL, (OWN, OWN, 1 - h))
        start_level(q, 1, 1 - h)

    rest, every, near_two = pl.ds(UP, 3), pl.ds(OWN, 4), pl.ds(UP, 2)

    def near(q, which):
        level = (h, 1 - h)[which]
        receive(q, RING1 + which * 3, (OWN, DOWN, level))
        receive(q, RING1 + which * 3 + 1, (OWN, UP, level))
        receive(q, RING1 + which * 3 + 2, (OWN, FAR, level))
        send(q, RING2_REST + which * 2, (OWN, rest, level), (DOWN, rest, level), second_up)
        send(q, RING2_REST + which * 2 + 1, (OWN, rest, level), (UP, rest, level), second_down)
        if which:
            send(q, CROSS, (OWN,), (OWN,), sibling)

    def arrive(q, which, way):
        side, level = (DOWN, UP)[way], (h, 1 - h)[which]
        receive(q, RING2 + which * 2 + way, (side, OWN, level))
        receive(q, RING2_REST + which * 2 + way, (side, rest, level))

    def early_columns(q):
        arrive(q, 0, 0)
        send(q, ACROSS, (DOWN, every, h), (FAR, every, h), second_up)

    def late_columns(q):
        arrive(q, 1, 1)
        send(q, ACROSS + 1, (UP, every, 1 - h), (FAR, every, 1 - h), second_down)
        arrive(q, 0, 1)
        arrive(q, 1, 0)
        send(q, CROSS + 1, (near_two,), (near_two,), sibling)

    def far_columns(q):
        receive(q, ACROSS, (FAR, every, h))
        receive(q, ACROSS + 1, (FAR, every, 1 - h))
        send(q, CROSS + 2, (FAR,), (FAR,), sibling)

    def complete(q):
        receive(q, CROSS, (OWN,))
        receive(q, CROSS + 1, (near_two,))
        receive(q, CROSS + 2, (FAR,))

    def label(row, side):
        return irreps_ref[slab_ref[row, side]]

    target_label = label(0, 0) + label(0, 1)

    def gate(panel, i):
        row = virt * 2 + panel + 1
        parity = lax.rem(label(row, 0) + label(row, 1) + target_label, 2)
        return (screen_ref[i, panel] * (1 - parity)).astype(jnp.float32)

    def unrolled(one, start, stop):
        def step(m, carry):
            for n in range(4):
                one(m * 4 + n)
            return carry

        lax.fori_loop(start // 4, stop // 4, step, 0)

    def gate_part(panel, i, start, stop):
        level = gate(panel, i)

        def one(m):
            lanes = pl.ds(pl.multiple_of(m * LANES, LANES), LANES)
            block_rows = amps[panel, 0, i, :, lanes].astype(jnp.float32) * level
            amps[panel, 0, i, :, lanes] = block_rows.astype(jnp.bfloat16)
            turned[lanes, :] = block_rows.T

        unrolled(one, start, stop)

    def flip_part(panel, i, start, stop):
        def one(m):
            even = turned[pl.ds(2 * m, TILE, stride=TILE), :]
            odd = turned[pl.ds(2 * m + 1, TILE, stride=TILE), :]
            lanes = pl.ds(pl.multiple_of(m * LANES, LANES), LANES)
            both = jnp.concatenate([even, odd], axis=0).T
            amps[1 - panel, 1, i, :, lanes] = both.astype(jnp.bfloat16)

        unrolled(one, start, stop)

    parts = []
    for panel in range(2):
        for i in range(2):
            for start in (0, 16):
                parts.append((gate_part, panel, i, start))
            for start in (0, 16):
                parts.append((flip_part, panel, i, start))
    loaded = set()

    def prepare(count):
        for _ in range(count):
            if not parts:
                return
            part, panel, i, start = parts.pop(0)
            if (panel, i) not in loaded:
                loaded.add((panel, i))
                loads[panel, i].wait()
            part(panel, i, start, start + 16)

    def place(position, centre):
        distance = lax.rem(position - centre + 4, 4)
        return distance + distance // 2 - 2 * (distance // 3)

    def multiply(q, panel, kinds):
        def step(at_x, carry):
            cells = []
            for level in range(2):
                for at_y in range(4):
                    near_x, near_y = place(at_x, x), place(at_y, y)
                    cells.append(panels[q, 0, near_y, near_x, level, panel])
                    cells.append(panels[q, 1, near_x, near_y, level, panel])
            right = jnp.concatenate(cells, axis=0)
            lanes = pl.ds(pl.multiple_of(at_x * 1024, 1024), 1024)
            left = amps[panel, kinds, :, :, lanes]
            count = left.shape[0]
            left = left.reshape(count * 256, 1024)
            product = jnp.dot(left, right, preferred_element_type=jnp.float32)
            partial[q, kinds] += product.reshape(count, 256, LANES)
            return carry

        lax.fori_loop(0, 4, step, 0)

    both = pl.ds(0, 2)

    sums = []

    def sum_copies(q, kind, source, device):
        return [
            pltpu.make_async_remote_copy(
                src_ref=mine.at[q, kind],
                dst_ref=theirs.at[source, kind],
                send_sem=sum_send.at[n, q, kind],
                recv_sem=sum_recv.at[n, source, kind],
                device_id=device,
                device_id_type=MESH,
            )
            for n, (mine, theirs) in enumerate(((coded, arrived), (scales, arrived_scales)))
        ]

    def pass_on(q):
        for kind in (1, 0):
            for i in range(2):
                values = partial[q, kind, i * 128:(i + 1) * 128]
                top = jnp.maximum(jnp.max(jnp.abs(values), axis=0, keepdims=True), 1e-33)
                steps = jnp.round(values * (STEPS / top))
                coded[q, kind, i * 128:(i + 1) * 128] = steps.astype(jnp.int32).astype(jnp.int16)
                scales[q, kind, i] = jnp.broadcast_to(top * (1 / STEPS), (8, LANES))
            for moved in sum_copies(q, kind, virt, (pair, blocks[q])):
                moved.start()
                sums.append(moved)

    others = [lax.rem(virt + step, 4) for step in range(1, 4)]

    def collect(kind, i):
        here = slice(i * 128, (i + 1) * 128)
        total = partial[3, kind, here]
        for other in others:
            steps = arrived[other, kind, here].astype(jnp.int32).astype(jnp.float32)
            total += steps * arrived_scales[other, kind, i][0:1]
        return total

    partial[...] = jnp.zeros((STAGES, 2, 256, LANES), jnp.float32)
    for q in range(STAGES):
        begin(q)
    prepare(4)
    begin_other(0)
    near(0, 0)
    prepare(1)
    begin_other(1)
    near(1, 0)
    prepare(1)
    begin_other(2)
    near(2, 0)
    begin_other(3)
    near(3, 0)
    prepare(2)
    near(0, 1)
    prepare(1)
    near(1, 1)
    early_columns(0)
    prepare(1)
    near(2, 1)
    early_columns(1)
    prepare(1)
    near(3, 1)
    early_columns(2)
    prepare(1)
    late_columns(0)
    prepare(1)
    early_columns(3)
    prepare(1)
    late_columns(1)
    prepare(len(parts))
    far_columns(0)
    late_columns(2)
    far_columns(1)
    complete(0)
    multiply(0, 0, both)
    late_columns(3)
    multiply(0, 1, both)
    pass_on(0)
    far_columns(2)
    complete(1)
    multiply(1, 0, both)
    far_columns(3)
    multiply(1, 1, both)
    pass_on(1)
    complete(2)
    multiply(2, 0, both)
    multiply(2, 1, both)
    pass_on(2)
    complete(3)
    multiply(3, 0, pl.ds(1, 1))
    multiply(3, 1, pl.ds(1, 1))

    for other in others:
        for moved in sum_copies(3, 1, other, along[0]):
            moved.wait_recv()
    for i in range(2):
        mirror_sum[i * 128:(i + 1) * 128] = collect(1, i)
    for which in range(2):
        for i in range(2):
            for j in range(2):
                rows = mirror_sum[pl.ds(i * 128 + which * 2 + j, 32, stride=4), :]
                tiles_out[pl.ds(which * 4 + i * 2 + j, 32, stride=8), :] = rows

    def tile_copy(target):
        return pltpu.make_async_remote_copy(
            src_ref=tiles_out.at[pl.ds(pl.multiple_of((target // 2) * 8, 8), 8)],
            dst_ref=tiles_in.at[pl.ds(pl.multiple_of(pair * 8, 8), 8)],
            send_sem=tile_send,
            recv_sem=tile_recv,
            device_id=(target, virt),
            device_id_type=MESH,
        )

    def exchange(step, carry):
        tile_copy(lax.rem(pair + step, 64)).start()
        return carry

    lax.fori_loop(1, 64, exchange, 0)
    tiles_in[pl.ds(pl.multiple_of(pair * 8, 8), 8), :] = tiles_out[
        pl.ds(pl.multiple_of((pair // 2) * 8, 8), 8), :
    ]
    multiply(3, 0, pl.ds(0, 1))
    multiply(3, 1, pl.ds(0, 1))
    for other in others:
        for moved in sum_copies(3, 0, other, along[0]):
            moved.wait_recv()
    for i in range(2):
        partial[3, 0, i * 128:(i + 1) * 128] = collect(0, i)

    everything = pltpu.make_async_remote_copy(
        src_ref=tiles_in.at[pl.ds(0, 63 * 8)],
        dst_ref=tiles_in.at[pl.ds(0, 63 * 8)],
        send_sem=tile_send,
        recv_sem=tile_recv,
        device_id=(lax.rem(pair + 1, 64), virt),
        device_id_type=MESH,
    )
    everything.wait_recv()
    for i in range(2):
        for j in range(2):
            direct = partial[3, 0, pl.ds(i * 128 + j, 64, stride=2), :]
            mirrored = tiles_in[pl.ds(core * 4 + j * 2 + i, 64, stride=8), :]
            result[pl.ds(i * 128 + j, 64, stride=2), :] = 0.5 * (direct + mirrored)
    out_ref[...] = result[...].astype(jnp.bfloat16).reshape(2, 128, LANES)

    everything.wait_send()
    for moved in sums:
        moved.wait_send()
    for moved in sent:
        moved.wait_send()


def body(amplitudes, integrals, screen, irreps, slab_index):
    rows = amplitudes.transpose(2, 0, 1, 3)
    smem = pl.BlockSpec(memory_space=pltpu.SMEM)
    anywhere = pl.BlockSpec(memory_space=pl.ANY)
    vmem = pl.BlockSpec(memory_space=pltpu.VMEM)
    dma, f32, bf16, i16 = pltpu.SemaphoreType.DMA, jnp.float32, jnp.bfloat16, jnp.int16
    return pl.pallas_call(
        kernel,
        out_shape=jax.ShapeDtypeStruct((2, 128, LANES), bf16),
        in_specs=[smem, smem, smem, anywhere, anywhere],
        out_specs=vmem,
        scratch_shapes=[
            pltpu.VMEM((STAGES, 2, 4, 4, 2, 2, TILE, LANES), bf16),
            pltpu.VMEM((2, 2, 2, 128, 4096), bf16),
            pltpu.VMEM((4096, 128), f32),
            pltpu.VMEM((STAGES, 2, 256, LANES), f32),
            pltpu.VMEM((STAGES, 2, 256, LANES), i16),
            pltpu.VMEM((STAGES, 2, 2, 8, LANES), f32),
            pltpu.VMEM((4, 2, 256, LANES), i16),
            pltpu.VMEM((4, 2, 2, 8, LANES), f32),
            pltpu.VMEM((256, LANES), f32),
            pltpu.VMEM((32 * 8, LANES), f32),
            pltpu.VMEM((64 * 8, LANES), f32),
            pltpu.VMEM((256, LANES), f32),
            dma((STAGES,)),
            dma((4,)),
            dma((STAGES, COPIES)),
            dma((STAGES, COPIES)),
            dma((2, STAGES, 2)),
            dma((2, 4, 2)),
            dma,
            dma,
        ],
        compiler_params=pltpu.CompilerParams(
            collective_id=0, has_side_effects=True, vmem_limit_bytes=40 * 1024 * 1024
        ),
        cost_estimate=pl.CostEstimate(
            flops=2 * 512 * 8192 * 512, bytes_accessed=5 << 20, transcendentals=0
        ),
    )(slab_index, irreps, screen, integrals, rows)


def solution(mesh):
    in_specs = (P("pair", None, "virt", None), P("virt", "pair", None), P("pair", "virt"), P(), P())
    out_specs = P("pair", None, "virt")
    return jax.shard_map(body, mesh=mesh, in_specs=in_specs, out_specs=out_specs, check_vma=False)
```

```python
import jax
import jax.numpy as jnp
from jax import lax
from jax.experimental import pallas as pl
from jax.experimental.pallas import tpu as pltpu
from jax.sharding import PartitionSpec as P

TILE = 64
STAGES = 2
BLOCKS = 4
LANES = 128
MESH = pl.DeviceIdType.MESH

RING1, RING2, RING2_REST, ACROSS, CROSS, LEVEL = 0, 6, 10, 14, 16, 19
COPIES = 20
STEPS = 32000.0
OWN, UP, DOWN, FAR = 0, 1, 2, 3


def pair_index(x, h, y, core):
    return ((x * 2 + h) * 4 + y) * 2 + core


def kernel(
    slab_ref, irreps_ref, screen_ref, own_ref, amp_ref, out_ref,
    panels, amps, turned, partial, coded, scales, arrived, arrived_scales, mirror_sum, tiles_out, tiles_in, result,
    local_sem, amp_sem, send_sem, recv_sem, sum_send, sum_recv, tile_send, tile_recv, own_sem,
):
    pair = lax.axis_index("pair")
    virt = lax.axis_index("virt")
    core = lax.rem(pair, 2)
    y = lax.rem(pair // 2, 4)
    h = lax.rem(pair // 8, 2)
    x = pair // 16
    first = x * (1 - core) + y * core
    second = y * (1 - core) + x * core

    def at(first_pos, second_pos, level, which_core):
        px = first_pos * (1 - core) + second_pos * core
        py = second_pos * (1 - core) + first_pos * core
        return (pair_index(px, level, py, which_core), virt)

    def around(position, step):
        return lax.rem(position + step, 4)

    first_up = at(around(first, 1), second, h, core)
    first_down = at(around(first, 3), second, h, core)
    first_far = at(around(first, 2), second, h, core)
    second_up = at(first, around(second, 1), h, core)
    second_down = at(first, around(second, 3), h, core)
    sibling = at(first, second, h, 1 - core)
    opposite = at(first, second, 1 - h, core)
    blocks = (3 * (1 - virt // 2), lax.rem(2 + 3 * virt, 5), 1 + lax.rem(virt, 2), virt)

    loads = {}
    for panel in range(2):
        for i in range(2):
            loads[panel, i] = pltpu.make_async_copy(
                amp_ref.at[panel, i], amps.at[panel, 0, i], amp_sem.at[panel * 2 + i]
            )
    local = {}
    for n in range(BLOCKS):
        columns = pl.ds(pl.multiple_of(blocks[n] * LANES, LANES), LANES)
        local[n] = pltpu.make_async_copy(
            own_ref.at[:, :, columns],
            panels.at[n // 2, core, OWN, OWN, h, :, :, pl.ds(n % 2 * LANES, LANES)],
            local_sem.at[n],
        )
        local[n].start()
    for load in loads.values():
        load.start()

    barrier = pltpu.get_barrier_semaphore()
    along = [(pair, lax.rem(virt + step, 4)) for step in range(1, 4)]
    for device in [first_up, first_down, first_far, second_up, second_down, sibling, opposite] + along:
        pl.semaphore_signal(barrier, inc=1, device_id=device, device_id_type=MESH)
    pl.semaphore_wait(barrier, 10)

    sent = []

    def copy(q, number, source, target, device):
        return pltpu.make_async_remote_copy(
            src_ref=panels.at[(q, core) + source],
            dst_ref=panels.at[(q, core) + target],
            send_sem=send_sem.at[q, number],
            recv_sem=recv_sem.at[q, number],
            device_id=device,
            device_id_type=MESH,
        )

    def send(q, number, source, target, device):
        moved = copy(q, number, source, target, device)
        moved.start()
        sent.append(moved)

    def receive(q, number, target):
        copy(q, number, target, target, sibling).wait_recv()

    def start_level(q, which, level):
        here = (OWN, OWN, level)
        send(q, RING1 + which * 3, here, (OWN, DOWN, level), first_up)
        send(q, RING1 + which * 3 + 1, here, (OWN, UP, level), first_down)
        send(q, RING1 + which * 3 + 2, here, (OWN, FAR, level), first_far)
        send(q, RING2 + which * 2, here, (DOWN, OWN, level), second_up)
        send(q, RING2 + which * 2 + 1, here, (UP, OWN, level), second_down)

    def begin(q):
        local[2 * q].wait()
        local[2 * q + 1].wait()
        send(q, LEVEL, (OWN, OWN, h), (OWN, OWN, h), opposite)
        start_level(q, 0, h)

    def begin_other(q):
        receive(q, LEVEL, (OWN, OWN, 1 - h))
        start_level(q, 1, 1 - h)

    rest, every, near_two = pl.ds(UP, 3), pl.ds(OWN, 4), pl.ds(UP, 2)

    def near(q, which):
        level = (h, 1 - h)[which]
        receive(q, RING1 + which * 3, (OWN, DOWN, level))
        receive(q, RING1 + which * 3 + 1, (OWN, UP, level))
        receive(q, RING1 + which * 3 + 2, (OWN, FAR, level))
        send(q, RING2_REST + which * 2, (OWN, rest, level), (DOWN, rest, level), second_up)
        send(q, RING2_REST + which * 2 + 1, (OWN, rest, level), (UP, rest, level), second_down)
        if which:
            send(q, CROSS, (OWN,), (OWN,), sibling)

    def arrive(q, which, way):
        side, level = (DOWN, UP)[way], (h, 1 - h)[which]
        receive(q, RING2 + which * 2 + way, (side, OWN, level))
        receive(q, RING2_REST + which * 2 + way, (side, rest, level))

    def early_columns(q):
        arrive(q, 0, 0)
        send(q, ACROSS, (DOWN, every, h), (FAR, every, h), second_up)

    def late_columns(q):
        arrive(q, 1, 1)
        send(q, ACROSS + 1, (UP, every, 1 - h), (FAR, every, 1 - h), second_down)
        arrive(q, 0, 1)
        arrive(q, 1, 0)
        send(q, CROSS + 1, (near_two,), (near_two,), sibling)

    def far_columns(q):
        receive(q, ACROSS, (FAR, every, h))
        receive(q, ACROSS + 1, (FAR, every, 1 - h))
        send(q, CROSS + 2, (FAR,), (FAR,), sibling)

    def complete(q):
        receive(q, CROSS, (OWN,))
        receive(q, CROSS + 1, (near_two,))
        receive(q, CROSS + 2, (FAR,))

    def label(row, side):
        return irreps_ref[slab_ref[side, row]]

    target_label = label(0, 0) + label(0, 1)

    def gate(panel, i):
        row = virt * 2 + panel + 1
        parity = lax.rem(label(row, 0) + label(row, 1) + target_label, 2)
        return (screen_ref[i, panel] * (1 - parity)).astype(jnp.float32)

    def unrolled(one, start, stop):
        def step(m, carry):
            for n in range(8):
                one(m * 8 + n)
            return carry

        lax.fori_loop(start // 8, stop // 8, step, 0)

    def gate_part(panel, i, start, stop):
        level = gate(panel, i)

        def one(m):
            lanes = pl.ds(pl.multiple_of(m * LANES, LANES), LANES)
            block_rows = amps[panel, 0, i, :, lanes].astype(jnp.float32) * level
            amps[panel, 0, i, :, lanes] = block_rows.astype(jnp.bfloat16)
            turned[lanes, :] = block_rows.T

        unrolled(one, start, stop)

    def flip_part(panel, i, start, stop):
        def one(m):
            even = turned[pl.ds(2 * m, TILE, stride=TILE), :]
            odd = turned[pl.ds(2 * m + 1, TILE, stride=TILE), :]
            lanes = pl.ds(pl.multiple_of(m * LANES, LANES), LANES)
            both = jnp.concatenate([even, odd], axis=0).astype(jnp.bfloat16)
            amps[1 - panel, 1, i, :, lanes] = both.T

        unrolled(one, start, stop)

    parts = []
    for panel in range(2):
        for i in range(2):
            for start in (0, 16):
                parts.append((gate_part, panel, i, start))
            for start in (0, 16):
                parts.append((flip_part, panel, i, start))
    loaded = set()

    def prepare(count):
        for _ in range(count):
            if not parts:
                return
            part, panel, i, start = parts.pop(0)
            if (panel, i) not in loaded:
                loaded.add((panel, i))
                loads[panel, i].wait()
            part(panel, i, start, start + 16)

    def place(position, centre):
        distance = lax.rem(position - centre + 4, 4)
        return distance + distance // 2 - 2 * (distance // 3)

    def multiply(q, panel, kinds):
        def step(n, carry):
            cells = []
            for at_x in (2 * n, 2 * n + 1):
                for level in range(2):
                    for at_y in range(4):
                        near_x, near_y = place(at_x, x), place(at_y, y)
                        cells.append(panels[q, 0, near_y, near_x, level, panel])
                        cells.append(panels[q, 1, near_x, near_y, level, panel])
            right = jnp.concatenate(cells, axis=0)
            lanes = pl.ds(pl.multiple_of(n * 2048, 2048), 2048)
            left = amps[panel, kinds, :, :, lanes]
            count = left.shape[0]
            left = left.reshape(count * 256, 2048)
            product = jnp.dot(left, right, preferred_element_type=jnp.float32)
            for m in range(2):
                part = product[:, m * LANES:(m + 1) * LANES]
                partial[2 * q + m, kinds] += part.reshape(count, 256, LANES)
            return carry

        lax.fori_loop(0, 2, step, 0)

    both = pl.ds(0, 2)

    sums = []

    def sum_copies(q, kind, source, device):
        return [
            pltpu.make_async_remote_copy(
                src_ref=mine.at[q, kind],
                dst_ref=theirs.at[source, kind],
                send_sem=sum_send.at[n, q, kind],
                recv_sem=sum_recv.at[n, source, kind],
                device_id=device,
                device_id_type=MESH,
            )
            for n, (mine, theirs) in enumerate(((coded, arrived), (scales, arrived_scales)))
        ]

    def pass_on(q, kinds=(1, 0)):
        for kind in kinds:
            for i in range(2):
                values = partial[q, kind, i * 128:(i + 1) * 128]
                top = jnp.maximum(jnp.max(jnp.abs(values), axis=0, keepdims=True), 1e-33)
                steps = jnp.round(values * (STEPS / top))
                coded[q, kind, i * 128:(i + 1) * 128] = steps.astype(jnp.int32).astype(jnp.int16)
                scales[q, kind, i] = jnp.broadcast_to(top * (1 / STEPS), (8, LANES))
            for moved in sum_copies(q, kind, virt, (pair, blocks[q])):
                moved.start()
                sums.append(moved)

    others = [lax.rem(virt + step, 4) for step in range(1, 4)]

    def collect(kind, i):
        here = slice(i * 128, (i + 1) * 128)
        total = partial[3, kind, here]
        for other in others:
            steps = arrived[other, kind, here].astype(jnp.int32).astype(jnp.float32)
            total += steps * arrived_scales[other, kind, i][0:1]
        return total

    begin(0)
    begin(1)
    partial[...] = jnp.zeros((BLOCKS, 2, 256, LANES), jnp.float32)
    prepare(4)
    begin_other(0)
    near(0, 0)
    prepare(2)
    begin_other(1)
    near(1, 0)
    prepare(2)
    near(0, 1)
    prepare(1)
    near(1, 1)
    early_columns(0)
    prepare(2)
    early_columns(1)
    prepare(2)
    late_columns(0)
    prepare(len(parts))
    late_columns(1)
    far_columns(0)
    mirrors, directs = pl.ds(1, 1), pl.ds(0, 1)
    complete(0)
    multiply(0, 0, mirrors)
    far_columns(1)
    multiply(0, 1, mirrors)
    pass_on(0, (1,))
    pass_on(1, (1,))
    complete(1)
    multiply(1, 0, mirrors)
    multiply(1, 1, mirrors)
    pass_on(2, (1,))
    multiply(0, 0, directs)
    multiply(0, 1, directs)
    pass_on(0, (0,))
    pass_on(1, (0,))
    multiply(1, 0, directs)
    multiply(1, 1, directs)
    pass_on(2, (0,))

    for other in others:
        for moved in sum_copies(3, 1, other, along[0]):
            moved.wait_recv()
    for i in range(2):
        mirror_sum[i * 128:(i + 1) * 128] = collect(1, i)
    for which in range(2):
        for i in range(2):
            for j in range(2):
                rows = mirror_sum[pl.ds(i * 128 + which * 2 + j, 32, stride=4), :]
                tiles_out[pl.ds(which * 4 + i * 2 + j, 32, stride=8), :] = rows

    def tile_copy(target):
        return pltpu.make_async_remote_copy(
            src_ref=tiles_out.at[pl.ds(pl.multiple_of(target * 4, 4), 4)],
            dst_ref=tiles_in.at[pl.ds(pl.multiple_of(pair * 4, 4), 4)],
            send_sem=tile_send,
            recv_sem=tile_recv,
            device_id=(target, virt),
            device_id_type=MESH,
        )

    def away(n):
        return n + n // 2 - 2 * (n // 3)

    def exchange(step, carry):
        left = 63 - step
        to_x = around(x, away(lax.rem(left // 8, 4)))
        to_y = around(y, away(lax.rem(left // 2, 4)))
        to_level = lax.rem(h + left // 32, 2)
        to_core = lax.rem(core + lax.rem(left, 2), 2)
        tile_copy(pair_index(to_x, to_level, to_y, to_core)).start()
        return carry

    lax.fori_loop(0, 63, exchange, 0)
    own_tile = pltpu.make_async_copy(
        tiles_out.at[pl.ds(pl.multiple_of(pair * 4, 4), 4)],
        tiles_in.at[pl.ds(pl.multiple_of(pair * 4, 4), 4)],
        own_sem,
    )
    own_tile.start()
    for other in others:
        for moved in sum_copies(3, 0, other, along[0]):
            moved.wait_recv()
    for i in range(2):
        partial[3, 0, i * 128:(i + 1) * 128] = collect(0, i)

    everything = pltpu.make_async_remote_copy(
        src_ref=tiles_in.at[pl.ds(0, 63 * 4)],
        dst_ref=tiles_in.at[pl.ds(0, 63 * 4)],
        send_sem=tile_send,
        recv_sem=tile_recv,
        device_id=(lax.rem(pair + 1, 64), virt),
        device_id_type=MESH,
    )
    own_tile.wait()
    everything.wait_recv()
    for i in range(2):
        for j in range(2):
            direct = partial[3, 0, pl.ds(i * 128 + j, 64, stride=2), :]
            mirrored = tiles_in[pl.ds(j * 2 + i, 64, stride=4), :]
            result[pl.ds(i * 128 + j, 64, stride=2), :] = 0.5 * (direct + mirrored)
    out_ref[...] = result[...].astype(jnp.bfloat16).reshape(2, 128, LANES)

    everything.wait_send()
    for moved in sums:
        moved.wait_send()
    for moved in sent:
        moved.wait_send()


def body(amplitudes, integrals, screen, irreps, slab_index):
    rows = amplitudes.transpose(2, 0, 1, 3)
    smem = pl.BlockSpec(memory_space=pltpu.SMEM)
    anywhere = pl.BlockSpec(memory_space=pl.ANY)
    vmem = pl.BlockSpec(memory_space=pltpu.VMEM)
    dma, f32, bf16, i16 = pltpu.SemaphoreType.DMA, jnp.float32, jnp.bfloat16, jnp.int16
    return pl.pallas_call(
        kernel,
        out_shape=jax.ShapeDtypeStruct((2, 128, LANES), bf16),
        in_specs=[smem, smem, smem, anywhere, anywhere],
        out_specs=vmem,
        scratch_shapes=[
            pltpu.VMEM((STAGES, 2, 4, 4, 2, 2, TILE, 2 * LANES), bf16),
            pltpu.VMEM((2, 2, 2, 128, 4096), bf16),
            pltpu.VMEM((4096, 128), f32),
            pltpu.VMEM((BLOCKS, 2, 256, LANES), f32),
            pltpu.VMEM((BLOCKS, 2, 256, LANES), i16),
            pltpu.VMEM((BLOCKS, 2, 2, 8, LANES), f32),
            pltpu.VMEM((4, 2, 256, LANES), i16),
            pltpu.VMEM((4, 2, 2, 8, LANES), f32),
            pltpu.VMEM((256, LANES), f32),
            pltpu.VMEM((32 * 8, LANES), f32),
            pltpu.VMEM((64 * 4, LANES), f32),
            pltpu.VMEM((256, LANES), f32),
            dma((BLOCKS,)),
            dma((4,)),
            dma((STAGES, COPIES)),
            dma((STAGES, COPIES)),
            dma((2, BLOCKS, 2)),
            dma((2, 4, 2)),
            dma,
            dma,
            dma,
        ],
        compiler_params=pltpu.CompilerParams(
            collective_id=0, has_side_effects=True, vmem_limit_bytes=40 * 1024 * 1024
        ),
        cost_estimate=pl.CostEstimate(
            flops=2 * 512 * 8192 * 512, bytes_accessed=5 << 20, transcendentals=0
        ),
    )(slab_index.T, irreps, screen, integrals, rows)


def solution(mesh):
    in_specs = (P("pair", None, "virt", None), P("virt", "pair", None), P("pair", "virt"), P(), P())
    out_specs = P("pair", None, "virt")
    return jax.shard_map(body, mesh=mesh, in_specs=in_specs, out_specs=out_specs, check_vma=False)
```

```python
import jax
import jax.numpy as jnp
from jax import lax
from jax.experimental import pallas as pl
from jax.experimental.pallas import tpu as pltpu
from jax.sharding import PartitionSpec as P

TILE = 64
STAGES = 2
BLOCKS = 4
LANES = 128
MESH = pl.DeviceIdType.MESH

RING1, RING2, RING2_REST, ACROSS, CROSS, LEVEL = 0, 6, 10, 14, 16, 19
COPIES = 20
STEPS = 32000.0
OWN, UP, DOWN, FAR = 0, 1, 2, 3


def pair_index(x, h, y, core):
    return ((x * 2 + h) * 4 + y) * 2 + core


def kernel(
    slab_ref, irreps_ref, screen_ref, own_ref, amp_ref, out_ref,
    panels, amps, turned, partial, coded, scales, arrived, arrived_scales, mirror_sum, tiles_out, tiles_in, result,
    local_sem, amp_sem, send_sem, recv_sem, sum_send, sum_recv, tile_send, tile_recv, own_sem,
):
    pair = lax.axis_index("pair")
    virt = lax.axis_index("virt")
    core = lax.rem(pair, 2)
    y = lax.rem(pair // 2, 4)
    h = lax.rem(pair // 8, 2)
    x = pair // 16
    first = x * (1 - core) + y * core
    second = y * (1 - core) + x * core

    def at(first_pos, second_pos, level, which_core):
        px = first_pos * (1 - core) + second_pos * core
        py = second_pos * (1 - core) + first_pos * core
        return (pair_index(px, level, py, which_core), virt)

    def around(position, step):
        return lax.rem(position + step, 4)

    first_up = at(around(first, 1), second, h, core)
    first_down = at(around(first, 3), second, h, core)
    first_far = at(around(first, 2), second, h, core)
    second_up = at(first, around(second, 1), h, core)
    second_down = at(first, around(second, 3), h, core)
    sibling = at(first, second, h, 1 - core)
    opposite = at(first, second, 1 - h, core)
    blocks = (3 * (1 - virt // 2), lax.rem(2 + 3 * virt, 5), 1 + lax.rem(virt, 2), virt)

    loads = {}
    for panel in range(2):
        for i in range(2):
            loads[panel, i] = pltpu.make_async_copy(
                amp_ref.at[panel, i], amps.at[panel, 0, i], amp_sem.at[panel * 2 + i]
            )
    local = {}
    for n in range(BLOCKS):
        columns = pl.ds(pl.multiple_of(blocks[n] * LANES, LANES), LANES)
        local[n] = pltpu.make_async_copy(
            own_ref.at[:, :, columns],
            panels.at[n // 2, core, OWN, OWN, h, :, :, pl.ds(n % 2 * LANES, LANES)],
            local_sem.at[n],
        )
        local[n].start()
    for load in loads.values():
        load.start()

    barrier = pltpu.get_barrier_semaphore()
    along = [(pair, lax.rem(virt + step, 4)) for step in range(1, 4)]
    for device in [first_up, first_down, first_far, second_up, second_down, sibling, opposite] + along:
        pl.semaphore_signal(barrier, inc=1, device_id=device, device_id_type=MESH)
    pl.semaphore_wait(barrier, 10)

    sent = []

    def copy(q, number, source, target, device):
        return pltpu.make_async_remote_copy(
            src_ref=panels.at[(q, core) + source],
            dst_ref=panels.at[(q, core) + target],
            send_sem=send_sem.at[q, number],
            recv_sem=recv_sem.at[q, number],
            device_id=device,
            device_id_type=MESH,
        )

    def send(q, number, source, target, device):
        moved = copy(q, number, source, target, device)
        moved.start()
        sent.append(moved)

    def receive(q, number, target):
        copy(q, number, target, target, sibling).wait_recv()

    def start_level(q, which, level):
        here = (OWN, OWN, level)
        send(q, RING1 + which * 3, here, (OWN, DOWN, level), first_up)
        send(q, RING1 + which * 3 + 1, here, (OWN, UP, level), first_down)
        send(q, RING1 + which * 3 + 2, here, (OWN, FAR, level), first_far)
        send(q, RING2 + which * 2, here, (DOWN, OWN, level), second_up)
        send(q, RING2 + which * 2 + 1, here, (UP, OWN, level), second_down)

    def begin(q):
        local[2 * q].wait()
        local[2 * q + 1].wait()
        send(q, LEVEL, (OWN, OWN, h), (OWN, OWN, h), opposite)
        start_level(q, 0, h)

    def begin_other(q):
        receive(q, LEVEL, (OWN, OWN, 1 - h))
        start_level(q, 1, 1 - h)

    rest, every, near_two = pl.ds(UP, 3), pl.ds(OWN, 4), pl.ds(UP, 2)

    def near(q, which):
        level = (h, 1 - h)[which]
        receive(q, RING1 + which * 3, (OWN, DOWN, level))
        receive(q, RING1 + which * 3 + 1, (OWN, UP, level))
        receive(q, RING1 + which * 3 + 2, (OWN, FAR, level))
        send(q, RING2_REST + which * 2, (OWN, rest, level), (DOWN, rest, level), second_up)
        send(q, RING2_REST + which * 2 + 1, (OWN, rest, level), (UP, rest, level), second_down)
        if which:
            send(q, CROSS, (OWN,), (OWN,), sibling)

    def arrive(q, which, way):
        side, level = (DOWN, UP)[way], (h, 1 - h)[which]
        receive(q, RING2 + which * 2 + way, (side, OWN, level))
        receive(q, RING2_REST + which * 2 + way, (side, rest, level))

    def early_columns(q):
        arrive(q, 0, 0)
        send(q, ACROSS, (DOWN, every, h), (FAR, every, h), second_up)

    def late_columns(q):
        arrive(q, 1, 1)
        send(q, ACROSS + 1, (UP, every, 1 - h), (FAR, every, 1 - h), second_down)
        arrive(q, 0, 1)
        arrive(q, 1, 0)
        send(q, CROSS + 1, (near_two,), (near_two,), sibling)

    def far_columns(q):
        receive(q, ACROSS, (FAR, every, h))
        receive(q, ACROSS + 1, (FAR, every, 1 - h))
        send(q, CROSS + 2, (FAR,), (FAR,), sibling)

    def complete(q):
        receive(q, CROSS, (OWN,))
        receive(q, CROSS + 1, (near_two,))
        receive(q, CROSS + 2, (FAR,))

    def label(row, side):
        return irreps_ref[slab_ref[side, row]]

    target_label = label(0, 0) + label(0, 1)

    def gate(panel, i):
        row = virt * 2 + panel + 1
        parity = lax.rem(label(row, 0) + label(row, 1) + target_label, 2)
        return (screen_ref[i, panel] * (1 - parity)).astype(jnp.float32)

    def unrolled(one, start, stop):
        def step(m, carry):
            for n in range(8):
                one(m * 8 + n)
            return carry

        lax.fori_loop(start // 8, stop // 8, step, 0)

    def gate_part(panel, i, start, stop):
        level = gate(panel, i)

        def one(m):
            lanes = pl.ds(pl.multiple_of(m * LANES, LANES), LANES)
            block_rows = amps[panel, 0, i, :, lanes].astype(jnp.float32) * level
            amps[panel, 0, i, :, lanes] = block_rows.astype(jnp.bfloat16)
            turned[lanes, :] = block_rows.T

        unrolled(one, start, stop)

    def flip_part(panel, i, start, stop):
        def one(m):
            even = turned[pl.ds(2 * m, TILE, stride=TILE), :]
            odd = turned[pl.ds(2 * m + 1, TILE, stride=TILE), :]
            lanes = pl.ds(pl.multiple_of(m * LANES, LANES), LANES)
            both = jnp.concatenate([even, odd], axis=0).astype(jnp.bfloat16)
            amps[1 - panel, 1, i, :, lanes] = both.T

        unrolled(one, start, stop)

    parts = []
    for panel in range(2):
        for i in range(2):
            for start in (0, 16):
                parts.append((gate_part, panel, i, start))
            for start in (0, 16):
                parts.append((flip_part, panel, i, start))
    loaded = set()

    def prepare(count):
        for _ in range(count):
            if not parts:
                return
            part, panel, i, start = parts.pop(0)
            if (panel, i) not in loaded:
                loaded.add((panel, i))
                loads[panel, i].wait()
            part(panel, i, start, start + 16)

    def place(position, centre):
        distance = lax.rem(position - centre + 4, 4)
        return distance + distance // 2 - 2 * (distance // 3)

    def multiply(q, panel, kinds):
        def step(n, carry):
            cells = []
            for at_x in (2 * n, 2 * n + 1):
                for level in range(2):
                    for at_y in range(4):
                        near_x, near_y = place(at_x, x), place(at_y, y)
                        cells.append(panels[q, 0, near_y, near_x, level, panel])
                        cells.append(panels[q, 1, near_x, near_y, level, panel])
            right = jnp.concatenate(cells, axis=0)
            lanes = pl.ds(pl.multiple_of(n * 2048, 2048), 2048)
            left = amps[panel, kinds, :, :, lanes]
            count = left.shape[0]
            left = left.reshape(count * 256, 2048)
            product = jnp.dot(left, right, preferred_element_type=jnp.float32)
            for m in range(2):
                part = product[:, m * LANES:(m + 1) * LANES]
                partial[2 * q + m, kinds] += part.reshape(count, 256, LANES)
            return carry

        lax.fori_loop(0, 2, step, 0)

    both = pl.ds(0, 2)

    sums = []

    def sum_copies(q, kind, source, device):
        return [
            pltpu.make_async_remote_copy(
                src_ref=mine.at[q, kind],
                dst_ref=theirs.at[source, kind],
                send_sem=sum_send.at[n, q, kind],
                recv_sem=sum_recv.at[n, source, kind],
                device_id=device,
                device_id_type=MESH,
            )
            for n, (mine, theirs) in enumerate(((coded, arrived), (scales, arrived_scales)))
        ]

    def pass_on(q, kinds=(1, 0)):
        for kind in kinds:
            for i in range(2):
                values = partial[q, kind, i * 128:(i + 1) * 128]
                top = jnp.maximum(jnp.max(jnp.abs(values), axis=0, keepdims=True), 1e-33)
                steps = jnp.round(values * (STEPS / top))
                coded[q, kind, i * 128:(i + 1) * 128] = steps.astype(jnp.int32).astype(jnp.int16)
                scales[q, kind, i] = jnp.broadcast_to(top * (1 / STEPS), (8, LANES))
            for moved in sum_copies(q, kind, virt, (pair, blocks[q])):
                moved.start()
                sums.append(moved)

    others = [lax.rem(virt + step, 4) for step in range(1, 4)]

    def collect(kind, i):
        here = slice(i * 128, (i + 1) * 128)
        total = partial[3, kind, here]
        for other in others:
            steps = arrived[other, kind, here].astype(jnp.int32).astype(jnp.float32)
            total += steps * arrived_scales[other, kind, i][0:1]
        return total

    begin(0)
    begin(1)
    partial[...] = jnp.zeros((BLOCKS, 2, 256, LANES), jnp.float32)
    prepare(3)
    near(0, 0)
    near(1, 0)
    begin_other(0)
    begin_other(1)
    prepare(3)
    near(0, 1)
    early_columns(0)
    prepare(2)
    near(1, 1)
    early_columns(1)
    prepare(2)
    late_columns(0)
    prepare(len(parts))
    late_columns(1)
    far_columns(0)
    mirrors, directs = pl.ds(1, 1), pl.ds(0, 1)
    complete(0)
    multiply(0, 0, mirrors)
    far_columns(1)
    multiply(0, 1, mirrors)
    pass_on(0, (1,))
    pass_on(1, (1,))
    complete(1)
    multiply(1, 0, mirrors)
    multiply(1, 1, mirrors)
    pass_on(2, (1,))
    multiply(0, 0, directs)
    multiply(0, 1, directs)
    pass_on(0, (0,))
    pass_on(1, (0,))
    multiply(1, 0, directs)
    multiply(1, 1, directs)
    pass_on(2, (0,))

    for other in others:
        for moved in sum_copies(3, 1, other, along[0]):
            moved.wait_recv()
    for i in range(2):
        mirror_sum[i * 128:(i + 1) * 128] = collect(1, i)
    for which in range(2):
        for i in range(2):
            for j in range(2):
                rows = mirror_sum[pl.ds(i * 128 + which * 2 + j, 32, stride=4), :]
                tiles_out[pl.ds(which * 4 + i * 2 + j, 32, stride=8), :] = rows

    def tile_copy(target):
        return pltpu.make_async_remote_copy(
            src_ref=tiles_out.at[pl.ds(pl.multiple_of(target * 4, 4), 4)],
            dst_ref=tiles_in.at[pl.ds(pl.multiple_of(pair * 4, 4), 4)],
            send_sem=tile_send,
            recv_sem=tile_recv,
            device_id=(target, virt),
            device_id_type=MESH,
        )

    def away(n):
        return n + n // 2 - 2 * (n // 3)

    def exchange(step, carry):
        left = 63 - step
        to_x = around(x, away(lax.rem(left // 8, 4)))
        to_y = around(y, away(lax.rem(left // 2, 4)))
        to_level = lax.rem(h + left // 32, 2)
        to_core = lax.rem(core + lax.rem(left, 2), 2)
        tile_copy(pair_index(to_x, to_level, to_y, to_core)).start()
        return carry

    lax.fori_loop(0, 63, exchange, 0)
    own_tile = pltpu.make_async_copy(
        tiles_out.at[pl.ds(pl.multiple_of(pair * 4, 4), 4)],
        tiles_in.at[pl.ds(pl.multiple_of(pair * 4, 4), 4)],
        own_sem,
    )
    own_tile.start()
    for other in others:
        for moved in sum_copies(3, 0, other, along[0]):
            moved.wait_recv()
    for i in range(2):
        partial[3, 0, i * 128:(i + 1) * 128] = collect(0, i)

    everything = pltpu.make_async_remote_copy(
        src_ref=tiles_in.at[pl.ds(0, 63 * 4)],
        dst_ref=tiles_in.at[pl.ds(0, 63 * 4)],
        send_sem=tile_send,
        recv_sem=tile_recv,
        device_id=(lax.rem(pair + 1, 64), virt),
        device_id_type=MESH,
    )
    own_tile.wait()
    everything.wait_recv()
    for i in range(2):
        for j in range(2):
            direct = partial[3, 0, pl.ds(i * 128 + j, 64, stride=2), :]
            mirrored = tiles_in[pl.ds(j * 2 + i, 64, stride=4), :]
            result[pl.ds(i * 128 + j, 64, stride=2), :] = 0.5 * (direct + mirrored)
    out_ref[...] = result[...].astype(jnp.bfloat16).reshape(2, 128, LANES)

    everything.wait_send()
    for moved in sums:
        moved.wait_send()
    for moved in sent:
        moved.wait_send()


def body(amplitudes, integrals, screen, irreps, slab_index):
    rows = amplitudes.transpose(2, 0, 1, 3)
    smem = pl.BlockSpec(memory_space=pltpu.SMEM)
    anywhere = pl.BlockSpec(memory_space=pl.ANY)
    vmem = pl.BlockSpec(memory_space=pltpu.VMEM)
    dma, f32, bf16, i16 = pltpu.SemaphoreType.DMA, jnp.float32, jnp.bfloat16, jnp.int16
    return pl.pallas_call(
        kernel,
        out_shape=jax.ShapeDtypeStruct((2, 128, LANES), bf16),
        in_specs=[smem, smem, smem, anywhere, anywhere],
        out_specs=vmem,
        scratch_shapes=[
            pltpu.VMEM((STAGES, 2, 4, 4, 2, 2, TILE, 2 * LANES), bf16),
            pltpu.VMEM((2, 2, 2, 128, 4096), bf16),
            pltpu.VMEM((4096, 128), f32),
            pltpu.VMEM((BLOCKS, 2, 256, LANES), f32),
            pltpu.VMEM((BLOCKS, 2, 256, LANES), i16),
            pltpu.VMEM((BLOCKS, 2, 2, 8, LANES), f32),
            pltpu.VMEM((4, 2, 256, LANES), i16),
            pltpu.VMEM((4, 2, 2, 8, LANES), f32),
            pltpu.VMEM((256, LANES), f32),
            pltpu.VMEM((32 * 8, LANES), f32),
            pltpu.VMEM((64 * 4, LANES), f32),
            pltpu.VMEM((256, LANES), f32),
            dma((BLOCKS,)),
            dma((4,)),
            dma((STAGES, COPIES)),
            dma((STAGES, COPIES)),
            dma((2, BLOCKS, 2)),
            dma((2, 4, 2)),
            dma,
            dma,
            dma,
        ],
        compiler_params=pltpu.CompilerParams(
            collective_id=0, has_side_effects=True, vmem_limit_bytes=40 * 1024 * 1024
        ),
        cost_estimate=pl.CostEstimate(
            flops=2 * 512 * 8192 * 512, bytes_accessed=5 << 20, transcendentals=0
        ),
    )(slab_index.T, irreps, screen, integrals, rows)


def solution(mesh):
    in_specs = (P("pair", None, "virt", None), P("virt", "pair", None), P("pair", "virt"), P(), P())
    out_specs = P("pair", None, "virt")
    return jax.shard_map(body, mesh=mesh, in_specs=in_specs, out_specs=out_specs, check_vma=False)
```

```python
import jax
import jax.numpy as jnp
from jax import lax
from jax.experimental import pallas as pl
from jax.experimental.pallas import tpu as pltpu
from jax.sharding import PartitionSpec as P

TILE = 64
STAGES = 2
BLOCKS = 4
LANES = 128
MESH = pl.DeviceIdType.MESH

RING1, RING2, RING2_REST, ACROSS, CROSS, LEVEL = 0, 6, 10, 14, 16, 19
COPIES = 20
STEPS = 32000.0
OWN, UP, DOWN, FAR = 0, 1, 2, 3


def pair_index(x, h, y, core):
    return ((x * 2 + h) * 4 + y) * 2 + core


def kernel(
    slab_ref, irreps_ref, screen_ref, own_ref, amp_ref, out_ref,
    panels, amps, turned, partial, coded, scales, arrived, arrived_scales, mirror_sum, tiles_out, tiles_in, result,
    local_sem, amp_sem, send_sem, recv_sem, sum_send, sum_recv, tile_send, tile_recv, own_sem,
):
    pair = lax.axis_index("pair")
    virt = lax.axis_index("virt")
    core = lax.rem(pair, 2)
    y = lax.rem(pair // 2, 4)
    h = lax.rem(pair // 8, 2)
    x = pair // 16
    first = x * (1 - core) + y * core
    second = y * (1 - core) + x * core

    def at(first_pos, second_pos, level, which_core):
        px = first_pos * (1 - core) + second_pos * core
        py = second_pos * (1 - core) + first_pos * core
        return (pair_index(px, level, py, which_core), virt)

    def around(position, step):
        return lax.rem(position + step, 4)

    first_up = at(around(first, 1), second, h, core)
    first_down = at(around(first, 3), second, h, core)
    first_far = at(around(first, 2), second, h, core)
    second_up = at(first, around(second, 1), h, core)
    second_down = at(first, around(second, 3), h, core)
    sibling = at(first, second, h, 1 - core)
    opposite = at(first, second, 1 - h, core)
    blocks = (3 * (1 - virt // 2), lax.rem(2 + 3 * virt, 5), 1 + lax.rem(virt, 2), virt)

    loads = {}
    for panel in range(2):
        for i in range(2):
            loads[panel, i] = pltpu.make_async_copy(
                amp_ref.at[panel, i], amps.at[panel, 0, i], amp_sem.at[panel * 2 + i]
            )
    local = {}
    for n in range(BLOCKS):
        columns = pl.ds(pl.multiple_of(blocks[n] * LANES, LANES), LANES)
        local[n] = pltpu.make_async_copy(
            own_ref.at[:, :, columns],
            panels.at[n // 2, core, OWN, OWN, h, :, :, pl.ds(n % 2 * LANES, LANES)],
            local_sem.at[n],
        )
        local[n].start()
    for load in loads.values():
        load.start()

    barrier = pltpu.get_barrier_semaphore()
    along = [(pair, lax.rem(virt + step, 4)) for step in range(1, 4)]
    for device in [first_up, first_down, first_far, second_up, second_down, sibling, opposite] + along:
        pl.semaphore_signal(barrier, inc=1, device_id=device, device_id_type=MESH)
    pl.semaphore_wait(barrier, 10)

    sent = []

    def copy(q, number, source, target, device):
        return pltpu.make_async_remote_copy(
            src_ref=panels.at[(q, core) + source],
            dst_ref=panels.at[(q, core) + target],
            send_sem=send_sem.at[q, number],
            recv_sem=recv_sem.at[q, number],
            device_id=device,
            device_id_type=MESH,
        )

    def send(q, number, source, target, device):
        moved = copy(q, number, source, target, device)
        moved.start()
        sent.append(moved)

    def receive(q, number, target):
        copy(q, number, target, target, sibling).wait_recv()

    def start_level(q, which, level):
        here = (OWN, OWN, level)
        send(q, RING1 + which * 3, here, (OWN, DOWN, level), first_up)
        send(q, RING1 + which * 3 + 1, here, (OWN, UP, level), first_down)
        send(q, RING1 + which * 3 + 2, here, (OWN, FAR, level), first_far)
        send(q, RING2 + which * 2, here, (DOWN, OWN, level), second_up)
        send(q, RING2 + which * 2 + 1, here, (UP, OWN, level), second_down)

    def begin(q):
        local[2 * q].wait()
        local[2 * q + 1].wait()
        send(q, LEVEL, (OWN, OWN, h), (OWN, OWN, h), opposite)
        start_level(q, 0, h)

    def begin_other(q):
        receive(q, LEVEL, (OWN, OWN, 1 - h))
        start_level(q, 1, 1 - h)

    rest, every, near_two = pl.ds(UP, 3), pl.ds(OWN, 4), pl.ds(UP, 2)

    def near(q, which):
        level = (h, 1 - h)[which]
        receive(q, RING1 + which * 3, (OWN, DOWN, level))
        receive(q, RING1 + which * 3 + 1, (OWN, UP, level))
        receive(q, RING1 + which * 3 + 2, (OWN, FAR, level))
        send(q, RING2_REST + which * 2, (OWN, rest, level), (DOWN, rest, level), second_up)
        send(q, RING2_REST + which * 2 + 1, (OWN, rest, level), (UP, rest, level), second_down)
        if which:
            send(q, CROSS, (OWN,), (OWN,), sibling)

    def arrive(q, which, way):
        side, level = (DOWN, UP)[way], (h, 1 - h)[which]
        receive(q, RING2 + which * 2 + way, (side, OWN, level))
        receive(q, RING2_REST + which * 2 + way, (side, rest, level))

    def early_columns(q):
        arrive(q, 0, 0)
        send(q, ACROSS, (DOWN, every, h), (FAR, every, h), second_up)

    def late_columns(q):
        arrive(q, 1, 1)
        send(q, ACROSS + 1, (UP, every, 1 - h), (FAR, every, 1 - h), second_down)
        arrive(q, 0, 1)
        arrive(q, 1, 0)
        send(q, CROSS + 1, (near_two,), (near_two,), sibling)

    def far_columns(q):
        receive(q, ACROSS, (FAR, every, h))
        receive(q, ACROSS + 1, (FAR, every, 1 - h))
        send(q, CROSS + 2, (FAR,), (FAR,), sibling)

    def complete(q):
        receive(q, CROSS, (OWN,))
        receive(q, CROSS + 1, (near_two,))
        receive(q, CROSS + 2, (FAR,))

    def label(row, side):
        return irreps_ref[slab_ref[side, row]]

    target_label = label(0, 0) + label(0, 1)

    def gate(panel, i):
        row = virt * 2 + panel + 1
        parity = lax.rem(label(row, 0) + label(row, 1) + target_label, 2)
        return (screen_ref[i, panel] * (1 - parity)).astype(jnp.float32)

    def unrolled(one, start, stop):
        def step(m, carry):
            for n in range(8):
                one(m * 8 + n)
            return carry

        lax.fori_loop(start // 8, stop // 8, step, 0)

    def gate_part(panel, i, start, stop):
        level = gate(panel, i)

        def one(m):
            lanes = pl.ds(pl.multiple_of(m * LANES, LANES), LANES)
            block_rows = amps[panel, 0, i, :, lanes].astype(jnp.float32) * level
            amps[panel, 0, i, :, lanes] = block_rows.astype(jnp.bfloat16)
            turned[lanes, :] = block_rows.T

        unrolled(one, start, stop)

    def flip_part(panel, i, start, stop):
        def one(m):
            even = turned[pl.ds(2 * m, TILE, stride=TILE), :]
            odd = turned[pl.ds(2 * m + 1, TILE, stride=TILE), :]
            lanes = pl.ds(pl.multiple_of(m * LANES, LANES), LANES)
            both = jnp.concatenate([even, odd], axis=0).astype(jnp.bfloat16)
            amps[1 - panel, 1, i, :, lanes] = both.T

        unrolled(one, start, stop)

    parts = []
    for panel in range(2):
        for i in range(2):
            for start in (0, 16):
                parts.append((gate_part, panel, i, start))
            for start in (0, 16):
                parts.append((flip_part, panel, i, start))
    loaded = set()

    def prepare(count):
        for _ in range(count):
            if not parts:
                return
            part, panel, i, start = parts.pop(0)
            if (panel, i) not in loaded:
                loaded.add((panel, i))
                loads[panel, i].wait()
            part(panel, i, start, start + 16)

    def place(position, centre):
        distance = lax.rem(position - centre + 4, 4)
        return distance + distance // 2 - 2 * (distance // 3)

    def multiply(q, panel, kinds):
        def step(n, carry):
            cells = []
            for at_x in (2 * n, 2 * n + 1):
                for level in range(2):
                    for at_y in range(4):
                        near_x, near_y = place(at_x, x), place(at_y, y)
                        cells.append(panels[q, 0, near_y, near_x, level, panel])
                        cells.append(panels[q, 1, near_x, near_y, level, panel])
            right = jnp.concatenate(cells, axis=0)
            lanes = pl.ds(pl.multiple_of(n * 2048, 2048), 2048)
            left = amps[panel, kinds, :, :, lanes]
            count = left.shape[0]
            left = left.reshape(count * 256, 2048)
            product = jnp.dot(left, right, preferred_element_type=jnp.float32)
            for m in range(2):
                part = product[:, m * LANES:(m + 1) * LANES]
                partial[2 * q + m, kinds] += part.reshape(count, 256, LANES)
            return carry

        lax.fori_loop(0, 2, step, 0)

    both = pl.ds(0, 2)

    sums = []

    def sum_copies(q, kind, source, device):
        return [
            pltpu.make_async_remote_copy(
                src_ref=mine.at[q, kind],
                dst_ref=theirs.at[source, kind],
                send_sem=sum_send.at[n, q, kind],
                recv_sem=sum_recv.at[n, source, kind],
                device_id=device,
                device_id_type=MESH,
            )
            for n, (mine, theirs) in enumerate(((coded, arrived), (scales, arrived_scales)))
        ]

    def pass_on(q, kinds=(1, 0)):
        for kind in kinds:
            for i in range(2):
                values = partial[q, kind, i * 128:(i + 1) * 128]
                top = jnp.maximum(jnp.max(jnp.abs(values), axis=0, keepdims=True), 1e-33)
                steps = jnp.round(values * (STEPS / top))
                coded[q, kind, i * 128:(i + 1) * 128] = steps.astype(jnp.int32).astype(jnp.int16)
                scales[q, kind, i] = jnp.broadcast_to(top * (1 / STEPS), (8, LANES))
            for moved in sum_copies(q, kind, virt, (pair, blocks[q])):
                moved.start()
                sums.append(moved)

    others = [lax.rem(virt + step, 4) for step in range(1, 4)]

    def collect(kind, i):
        here = slice(i * 128, (i + 1) * 128)
        total = partial[3, kind, here]
        for other in others:
            steps = arrived[other, kind, here].astype(jnp.int32).astype(jnp.float32)
            total += steps * arrived_scales[other, kind, i][0:1]
        return total

    begin(0)
    begin(1)
    partial[...] = jnp.zeros((BLOCKS, 2, 256, LANES), jnp.float32)
    prepare(3)
    near(0, 0)
    near(1, 0)
    begin_other(0)
    begin_other(1)
    prepare(3)
    near(0, 1)
    early_columns(0)
    prepare(2)
    near(1, 1)
    early_columns(1)
    prepare(2)
    late_columns(0)
    prepare(len(parts))
    late_columns(1)
    far_columns(0)
    mirrors, directs = pl.ds(1, 1), pl.ds(0, 1)
    complete(0)
    multiply(0, 0, mirrors)
    far_columns(1)
    multiply(0, 1, mirrors)
    pass_on(0, (1,))
    pass_on(1, (1,))
    complete(1)
    multiply(1, 0, mirrors)
    multiply(1, 1, mirrors)
    pass_on(2, (1,))
    multiply(0, 0, directs)
    multiply(0, 1, directs)
    pass_on(0, (0,))
    pass_on(1, (0,))
    multiply(1, 0, directs)
    multiply(1, 1, directs)
    pass_on(2, (0,))

    for other in others:
        for moved in sum_copies(3, 1, other, along[0]):
            moved.wait_recv()
    for i in range(2):
        mirror_sum[i * 128:(i + 1) * 128] = collect(1, i)
    for which in range(2):
        for i in range(2):
            for j in range(2):
                rows = mirror_sum[pl.ds(i * 128 + which * 2 + j, 32, stride=4), :]
                tiles_out[pl.ds(which * 4 + i * 2 + j, 32, stride=8), :] = rows

    def tile_copy(target):
        return pltpu.make_async_remote_copy(
            src_ref=tiles_out.at[pl.ds(pl.multiple_of(target * 4, 4), 4)],
            dst_ref=tiles_in.at[pl.ds(pl.multiple_of(pair * 4, 4), 4)],
            send_sem=tile_send,
            recv_sem=tile_recv,
            device_id=(target, virt),
            device_id_type=MESH,
        )

    def away(n):
        return n + n // 2 - 2 * (n // 3)

    near_places = [around(y, step) * 2 + side for step in (2, 1, 3, 0) for side in (1 - core, core)]

    def exchange(step, carry):
        left = 7 - step
        far_place = (around(x, away(lax.rem(left, 4))) * 2 + lax.rem(h + left // 4, 2)) * 8
        for near_place in near_places:
            tile_copy(far_place + near_place).start()
        return carry

    lax.fori_loop(0, 7, exchange, 0)
    for near_place in near_places[:-1]:
        tile_copy((x * 2 + h) * 8 + near_place).start()
    own_tile = pltpu.make_async_copy(
        tiles_out.at[pl.ds(pl.multiple_of(pair * 4, 4), 4)],
        tiles_in.at[pl.ds(pl.multiple_of(pair * 4, 4), 4)],
        own_sem,
    )
    own_tile.start()
    for other in others:
        for moved in sum_copies(3, 0, other, along[0]):
            moved.wait_recv()
    for i in range(2):
        partial[3, 0, i * 128:(i + 1) * 128] = collect(0, i)

    everything = pltpu.make_async_remote_copy(
        src_ref=tiles_in.at[pl.ds(0, 63 * 4)],
        dst_ref=tiles_in.at[pl.ds(0, 63 * 4)],
        send_sem=tile_send,
        recv_sem=tile_recv,
        device_id=(lax.rem(pair + 1, 64), virt),
        device_id_type=MESH,
    )
    own_tile.wait()
    everything.wait_recv()
    for i in range(2):
        for j in range(2):
            direct = partial[3, 0, pl.ds(i * 128 + j, 64, stride=2), :]
            mirrored = tiles_in[pl.ds(j * 2 + i, 64, stride=4), :]
            result[pl.ds(i * 128 + j, 64, stride=2), :] = 0.5 * (direct + mirrored)
    out_ref[...] = result[...].astype(jnp.bfloat16).reshape(2, 128, LANES)

    everything.wait_send()
    for moved in sums:
        moved.wait_send()
    for moved in sent:
        moved.wait_send()


def body(amplitudes, integrals, screen, irreps, slab_index):
    rows = amplitudes.transpose(2, 0, 1, 3)
    smem = pl.BlockSpec(memory_space=pltpu.SMEM)
    anywhere = pl.BlockSpec(memory_space=pl.ANY)
    vmem = pl.BlockSpec(memory_space=pltpu.VMEM)
    dma, f32, bf16, i16 = pltpu.SemaphoreType.DMA, jnp.float32, jnp.bfloat16, jnp.int16
    return pl.pallas_call(
        kernel,
        out_shape=jax.ShapeDtypeStruct((2, 128, LANES), bf16),
        in_specs=[smem, smem, smem, anywhere, anywhere],
        out_specs=vmem,
        scratch_shapes=[
            pltpu.VMEM((STAGES, 2, 4, 4, 2, 2, TILE, 2 * LANES), bf16),
            pltpu.VMEM((2, 2, 2, 128, 4096), bf16),
            pltpu.VMEM((4096, 128), f32),
            pltpu.VMEM((BLOCKS, 2, 256, LANES), f32),
            pltpu.VMEM((BLOCKS, 2, 256, LANES), i16),
            pltpu.VMEM((BLOCKS, 2, 2, 8, LANES), f32),
            pltpu.VMEM((4, 2, 256, LANES), i16),
            pltpu.VMEM((4, 2, 2, 8, LANES), f32),
            pltpu.VMEM((256, LANES), f32),
            pltpu.VMEM((32 * 8, LANES), f32),
            pltpu.VMEM((64 * 4, LANES), f32),
            pltpu.VMEM((256, LANES), f32),
            dma((BLOCKS,)),
            dma((4,)),
            dma((STAGES, COPIES)),
            dma((STAGES, COPIES)),
            dma((2, BLOCKS, 2)),
            dma((2, 4, 2)),
            dma,
            dma,
            dma,
        ],
        compiler_params=pltpu.CompilerParams(
            collective_id=0, has_side_effects=True, vmem_limit_bytes=40 * 1024 * 1024
        ),
        cost_estimate=pl.CostEstimate(
            flops=2 * 512 * 8192 * 512, bytes_accessed=5 << 20, transcendentals=0
        ),
    )(slab_index.T, irreps, screen, integrals, rows)


def solution(mesh):
    in_specs = (P("pair", None, "virt", None), P("virt", "pair", None), P("pair", "virt"), P(), P())
    out_specs = P("pair", None, "virt")
    return jax.shard_map(body, mesh=mesh, in_specs=in_specs, out_specs=out_specs, check_vma=False)
```
